32 devices in a mesh: groups: 2 (over y), ep: 8 (over z, x), edp: 2 (over core).
Axes of the slice: x: 2, y: 2, z: 4, core: 2. Of those that a mesh axis runs over, the one named last changes fastest.
Arguments:
- hidden_in: bfloat16 [4096, 2048], P(('groups', 'ep', 'edp')), parts along dimension 0, may hold values from -6 to 6
- out_grad: bfloat16 [4096, 2048], P(('groups', 'ep', 'edp')), parts along dimension 0, may hold values from -0.59765625 to 0.59765625
- routes: int32 [4096, 2], P(('groups', 'ep', 'edp')), parts along dimension 0, may hold values from 0 to 7, all different within a row; in each aligned block of 128 rows (0 to 127, 128 to 255, ...) at most 64 rows name the same one
- probs: float32 [4096, 2], P(('groups', 'ep', 'edp')), parts along dimension 0, may hold values from 0.05 to 1
- w_gate: bfloat16 [8, 2048, 768], P('ep', 'edp'), may hold values from -0.125 to 0.125
- w_up: bfloat16 [8, 2048, 768], P('ep', 'edp'), may hold values from -0.125 to 0.125
- w_down: bfloat16 [8, 768, 2048], P('ep', 'edp'), may hold values from -0.21875 to 0.21875
Outputs:
- input_grad: bfloat16 [4096, 2048], P(('groups', 'ep', 'edp')), parts along dimension 0
- prob_grad: float32 [4096, 2], P(('groups', 'ep', 'edp')), parts along dimension 0
- gate_wgrad: bfloat16 [16, 2048, 768], P(('groups', 'ep'), 'edp'), parts along dimension 0
- up_wgrad: bfloat16 [16, 2048, 768], P(('groups', 'ep'), 'edp'), parts along dimension 0
- down_wgrad: bfloat16 [16, 768, 2048], P(('groups', 'ep'), 'edp'), parts along dimension 0
The draws below stay inside these ranges and needn't reach their ends.
There are 2 independent parts, one for each index of `groups`. The reference program is written for one: setup_inputs(seed, part) draws one part's arguments, and reference() takes and returns one part's arrays. A program takes and returns all parts, laid end to end along the dimension named above; an argument that names none is the same for every part. Nothing has to cross between parts.
Inputs may be any that keep to these rules, and one draw needn't show every extreme that they name: `routes`: each row names 2 different experts; among the rows of one device no expert is named more than 64 times.
All inputs are finite; a program needn't handle non-finite values.
Results may differ from the reference program's by a relative error of at most 0.015.
Values may be sent and summed in bfloat16 or wider, within the bound.
A program may use at most 128 MiB of HBM per device.

```python
import math
import jax
import jax.numpy as jnp
import numpy as np
from jax import lax

D = 2048
FF = 768
TOP = 2
TOK_DEV = 128
EXPERTS = 8
TOKENS = 2048
SEND_CAP = 64
N_EP = 8
N_EDP = 2


def levels(rng, shape, split, low, top_value):
    def one(axis_at, blocks):
        heights = jax.random.uniform(jax.random.fold_in(jax.random.fold_in(rng, 6), axis_at), (blocks,), jnp.float32, low / len(split), top_value / len(split))
        return jnp.repeat(jnp.exp(heights), shape[axis_at] // blocks).reshape((-1,) + (1,) * (len(shape) - axis_at - 1))

    level = one(*split[0])
    for cut in split[1:]:
        level = level * one(*cut)
    return level


def assign_block(rng, own, number, rows, count, top, most, skew):
    ranking = jax.random.permutation(rng, count)
    heavy_load, common = load_shares(count, rows * top, most, skew, True), load_shares(count, rows * top, most, skew, False)
    places = jnp.arange(count)

    def named(sizes, offset_by):
        used = int((sizes > 0).sum())
        fixed = max(1, used // 4)
        shifted = fixed + (places - fixed + offset_by * (used - fixed)) % max(1, count - fixed)
        return jnp.zeros((count,), jnp.int32).at[ranking[jnp.where(places < fixed, places, shifted)]].set(jnp.asarray(sizes, jnp.int32))

    sizes = jnp.where(number % 4 == 0, named(heavy_load, number // 4), named(common, number - number // 4 - 1))
    mixed = jax.random.permutation(jax.random.fold_in(own, 3), count)
    giver, taker = mixed[0:count // 2 * 2:2], mixed[1:count // 2 * 2:2]
    slack = jnp.minimum(sizes[giver] - 1, most - sizes[taker]) // 2
    slack = jnp.where((giver == ranking[0]) | (taker == ranking[0]) | (sizes[taker] == 0), 0, jnp.maximum(slack, 0))
    shifted = jax.random.randint(jax.random.fold_in(own, 4), (count // 2,), 0, 1 << 20) % (slack + 1)
    sizes = sizes.at[giver].add(-shifted).at[taker].add(shifted)
    labels = jnp.searchsorted(jnp.cumsum(sizes), jnp.arange(rows * top), side="right").astype(jnp.int32)
    grid = labels.reshape(top, rows).T
    grid = grid[jax.random.permutation(jax.random.fold_in(own, 1), rows)]
    offset_by = jax.random.randint(jax.random.fold_in(own, 2), (rows, 1), 0, top)
    return jnp.take_along_axis(grid, (jnp.arange(top)[None, :] + offset_by) % top, axis=1)


def load_shares(count, total, reach, skew, full):
    weights = [(1 << 20) // math.isqrt(grade ** skew) + 1 for grade in range(1, count + 1)]
    largest = reach if full else min(reach, max(-(-total // count), total * weights[0] // sum(weights)))
    least = 1 if total - largest >= count - 1 else 0
    holding, spare = [largest] + [least] * (count - 1), total - largest - least * (count - 1)
    while spare > 0:
        movable = [i for i in range(1, count) if holding[i] < largest] or [i for i in range(1, count) if holding[i] < reach]
        mass, left = sum([weights[i] for i in movable]), spare
        for i in movable:
            extra = min(reach - holding[i], max(1, left * weights[i] // mass), spare)
            holding[i] = holding[i] + extra
            spare = spare - extra
    return np.array(holding)


def gaussian(own_key, shape, width, bound, shards=(), kind=jnp.bfloat16):
    loudness = levels(own_key, shape, shards, -0.22, 0.18) if shards else 1.0
    result = jax.random.normal(own_key, shape, jnp.float32) * width * loudness
    return jnp.minimum(jnp.maximum(result, -bound), bound).astype(kind)


def setup_inputs(seed: int = 0, part: int = 0) -> dict:
    key_list = jax.random.split(jax.random.key(seed), 8)
    part_splits = jax.random.split(jax.random.fold_in(key_list[7], part), 8)
    hidden_in = gaussian(part_splits[0], (TOKENS, D), 1.0, 6.0, ((0, 16),))
    out_grad = gaussian(part_splits[1], (TOKENS, D), 0.1, 0.59765625, ((0, 16),))
    routes_keys = jax.random.split(jax.random.fold_in(part_splits[2], 1), TOKENS // TOK_DEV)
    routes_turns = jax.random.permutation(jax.random.fold_in(part_splits[2], 3), TOKENS // TOK_DEV)
    routes = jax.vmap(lambda own, number: assign_block(jax.random.fold_in(part_splits[2], 2), own, number, TOK_DEV, EXPERTS, TOP, SEND_CAP, 2))(routes_keys, routes_turns).reshape((TOKENS, TOP))
    probs = jnp.clip(0.05 + 0.95 * jax.random.uniform(part_splits[3], (TOKENS, TOP), jnp.float32) ** levels(part_splits[3], (TOKENS, TOP), ((0, 16),), -0.2, 0.2), 0.05, 1.0)
    w_gate = gaussian(key_list[4], (EXPERTS, D, FF), D ** -0.5, 0.125, ((0, 8), (1, 2)))
    w_up = gaussian(key_list[5], (EXPERTS, D, FF), D ** -0.5, 0.125, ((0, 8), (1, 2)))
    w_down = gaussian(key_list[6], (EXPERTS, FF, D), FF ** -0.5, 0.21875, ((0, 8), (1, 2)))
    return dict(hidden_in=hidden_in, out_grad=out_grad, routes=routes, probs=probs, w_gate=w_gate, w_up=w_up, w_down=w_down)


def forward_part(rows_in, gate_full, up_full, down_full):
    gate = jnp.dot(rows_in, gate_full, preferred_element_type=jnp.float32)
    upper = jnp.dot(rows_in, up_full, preferred_element_type=jnp.float32)
    sigma = jax.nn.sigmoid(gate)
    active = gate * sigma
    hidden = (active * upper).astype(jnp.bfloat16)
    expert_out = jnp.dot(hidden, down_full, preferred_element_type=jnp.float32)
    return gate, upper, sigma, active, hidden, expert_out


def backward_part(state, rows_grad, weights_row, gate_full, up_full, down_full):
    gate, upper, sigma, active, hidden, expert_out = state
    grad_wide = rows_grad.astype(jnp.float32)
    prob_grad = jnp.sum(expert_out * grad_wide, axis=1)
    scaled = (weights_row[:, None] * grad_wide).astype(jnp.bfloat16)
    hidden_grad = lax.dot_general(scaled, down_full, (((1,), (1,)), ((), ())), preferred_element_type=jnp.float32)
    up_grad = (hidden_grad * active).astype(jnp.bfloat16)
    gate_grad = (hidden_grad * upper * sigma * (1.0 + gate * (1.0 - sigma))).astype(jnp.bfloat16)
    row_grad = lax.dot_general(gate_grad, gate_full, (((1,), (1,)), ((), ())), preferred_element_type=jnp.float32)
    row_grad = row_grad + lax.dot_general(up_grad, up_full, (((1,), (1,)), ((), ())), preferred_element_type=jnp.float32)
    return scaled, gate_grad, up_grad, row_grad.astype(jnp.bfloat16), prob_grad


def weight_terms(rows_in, hidden, scaled, gate_grad, up_grad):
    contract = (((0,), (0,)), ((), ()))
    gate_term = lax.dot_general(rows_in, gate_grad, contract, preferred_element_type=jnp.float32)
    up_term = lax.dot_general(rows_in, up_grad, contract, preferred_element_type=jnp.float32)
    down_term = lax.dot_general(hidden, scaled, contract, preferred_element_type=jnp.float32)
    return gate_term, up_term, down_term


def rounded(value):
    return lax.optimization_barrier(value.astype(jnp.bfloat16)).astype(jnp.float32)


def reference(hidden_in, out_grad, routes, probs, w_gate, w_up, w_down):
    blocks = N_EP * N_EDP
    slot_room = blocks * SEND_CAP
    block_routes = routes.reshape(blocks, TOK_DEV * TOP)
    onehot = (block_routes[:, :, None] == jnp.arange(EXPERTS, dtype=jnp.int32)[None, None, :]).astype(jnp.int32)
    running = jnp.cumsum(onehot, axis=1) - 1
    position = jnp.sum(running * onehot, axis=2)
    destination = (jnp.arange(blocks, dtype=jnp.int32)[:, None] * SEND_CAP + position).reshape(-1).astype(jnp.int32)
    flat_routes = block_routes.reshape(-1)
    token_ids = (jnp.arange(TOKENS * TOP, dtype=jnp.int32) // TOP).astype(jnp.int32)
    padded_in = jnp.concatenate([hidden_in, jnp.zeros((1, D), hidden_in.dtype)], axis=0)
    padded_grad = jnp.concatenate([out_grad, jnp.zeros((1, D), out_grad.dtype)], axis=0)
    probs_flat = probs.reshape(-1)

    def per_expert(expert):
        target = jnp.where(flat_routes == expert, destination, slot_room).astype(jnp.int32)
        index = jnp.full((slot_room,), TOKENS, jnp.int32).at[target].set(token_ids, mode="drop")
        weights_slot = jnp.zeros((slot_room,), probs.dtype).at[target].set(probs_flat, mode="drop")
        rows_in = padded_in[index].reshape(N_EP, N_EDP, SEND_CAP, D)
        rows_grad = padded_grad[index].reshape(N_EP, N_EDP, SEND_CAP, D)
        weights_slot = weights_slot.reshape(N_EP, N_EDP, SEND_CAP)
        gate_full, up_full, down_full = w_gate[expert], w_up[expert], w_down[expert]
        sums = None
        row_parts = []
        prob_parts = []
        for half in range(N_EDP):
            part_in = rows_in[:, half].reshape(N_EP * SEND_CAP, D)
            part_grad = rows_grad[:, half].reshape(N_EP * SEND_CAP, D)
            part_weights = weights_slot[:, half].reshape(N_EP * SEND_CAP)
            state = forward_part(part_in, gate_full, up_full, down_full)
            scaled, gate_grad, up_grad, row_grad, prob_grad = backward_part(state, part_grad, part_weights, gate_full, up_full, down_full)
            terms = weight_terms(part_in, state[4], scaled, gate_grad, up_grad)
            terms = tuple(rounded(term) for term in terms)
            sums = terms if sums is None else tuple(a + b for a, b in zip(sums, terms))
            row_parts.append(row_grad.reshape(N_EP, SEND_CAP, D))
            prob_parts.append(prob_grad.reshape(N_EP, SEND_CAP))
        slot_rows = jnp.stack(row_parts, axis=1).reshape(slot_room, D)
        slot_probs = jnp.stack(prob_parts, axis=1).reshape(slot_room)
        return (sums[0].astype(jnp.bfloat16), sums[1].astype(jnp.bfloat16), sums[2].astype(jnp.bfloat16), slot_rows, slot_probs)

    gate_wgrad, up_wgrad, down_wgrad, slot_rows, slot_probs = lax.map(per_expert, jnp.arange(EXPERTS, dtype=jnp.int32))
    picked_rows = slot_rows[flat_routes, destination]
    input_grad = jnp.sum(picked_rows.astype(jnp.float32).reshape(TOKENS, TOP, D), axis=1).astype(jnp.bfloat16)
    prob_grad = slot_probs[flat_routes, destination].reshape(TOKENS, TOP)
    return input_grad, prob_grad, gate_wgrad, up_wgrad, down_wgrad
```

```python
import jax
import jax.numpy as jnp
from jax import lax
from jax.sharding import PartitionSpec as P

F32 = jnp.float32
BF16 = jnp.bfloat16
LANE = 128


def dot(a, b, dims):
    return lax.dot_general(a, b, (dims, ((), ())), preferred_element_type=F32)


def routing(routes, probs, experts, cap):
    tok, top = routes.shape
    picks = routes[:, :, None] == jnp.arange(experts, dtype=jnp.int32)[None, None, :]
    chosen = jnp.any(picks, axis=1)
    weight = jnp.sum(jnp.where(picks, probs[:, :, None], 0.0), axis=1)
    order = jnp.arange(tok, dtype=jnp.int32)
    earlier = (order[:, None] > order[None, :]).astype(BF16)
    place = dot(earlier, chosen.astype(BF16), ((1,), (0,))).astype(jnp.int32)
    place = jnp.where(chosen, place, -1)
    slot = jnp.arange(cap, dtype=jnp.int32)
    select = place.T[:, None, :] == slot[None, :, None]
    return picks, select, weight


def local(hidden_in, out_grad, routes, probs, w_gate, w_up, w_down):
    tok, top = routes.shape
    width = hidden_in.shape[1]
    ep = lax.axis_size("ep")
    experts = ep * w_gate.shape[0]
    cap = max(8, 2 * tok * top // experts)
    rows = experts * cap
    picks, select, weight = routing(routes, probs, experts, cap)
    select_rows = select.reshape(rows, tok).astype(BF16)
    row_weight = jnp.sum(jnp.where(select, weight.T[:, None, :], 0.0), axis=2).reshape(rows, 1)
    send_in = dot(select_rows, hidden_in, ((1,), (0,))).astype(BF16)
    send_grad = dot(select_rows, out_grad, ((1,), (0,))).astype(BF16)
    send_grad = jnp.concatenate(
        [send_grad, jnp.broadcast_to(row_weight.astype(BF16), (rows, LANE))], axis=1
    )

    def swap(value):
        return lax.all_to_all(
            value.reshape(experts, cap, -1), "ep", split_axis=0, concat_axis=0, tiled=True
        ).reshape(rows, -1)

    gate_full, up_full, down_full = (
        lax.all_gather(w[0], "edp", axis=0, tiled=True) for w in (w_gate, w_up, w_down)
    )
    rows_in = swap(send_in)
    got = swap(send_grad)
    rows_grad = got[:, :width]
    p = got[:, width : width + 1].astype(F32)
    gate = dot(rows_in, gate_full, ((1,), (0,)))
    upper = dot(rows_in, up_full, ((1,), (0,)))
    sigma = jax.nn.sigmoid(gate)
    active = gate * sigma
    hidden = active * upper
    plain = dot(rows_grad, down_full, ((1,), (1,)))
    prob_grad = jnp.sum(hidden * plain, axis=1, keepdims=True)
    hidden_grad = plain * p
    up_grad = (hidden_grad * active).astype(BF16)
    gate_grad = (hidden_grad * upper * sigma * (1.0 + gate * (1.0 - sigma))).astype(BF16)
    scaled_hidden = (hidden * p).astype(BF16)
    row_grad = dot(gate_grad, gate_full, ((1,), (1,))) + dot(up_grad, up_full, ((1,), (1,)))
    row_grad = jnp.concatenate(
        [row_grad.astype(BF16), jnp.broadcast_to(prob_grad.astype(BF16), (rows, LANE))], axis=1
    )
    row_grad, gate_grad, up_grad, scaled_hidden = lax.optimization_barrier(
        (row_grad, gate_grad, up_grad, scaled_hidden)
    )
    back = swap(row_grad)
    input_grad = dot(select_rows, back[:, :width], ((0,), (0,))).astype(BF16)
    back_prob = back[:, width].astype(F32).reshape(experts, cap, 1)
    by_expert = jnp.sum(jnp.where(select, back_prob, 0.0), axis=1).T
    prob_out = jnp.sum(jnp.where(picks, by_expert[:, None, :], 0.0), axis=2)

    def share(a, b):
        term = dot(a, b, ((0,), (0,))).astype(BF16)
        return lax.psum_scatter(term, "edp", scatter_dimension=0, tiled=True)[None]

    return (
        input_grad,
        prob_out,
        share(rows_in, gate_grad),
        share(rows_in, up_grad),
        share(scaled_hidden, rows_grad),
    )


def solution(mesh):
    tokens = P(("groups", "ep", "edp"), None)
    weights = P("ep", "edp", None)
    grads = P(("groups", "ep"), "edp", None)
    return jax.shard_map(
        local,
        mesh=mesh,
        in_specs=(tokens,) * 4 + (weights,) * 3,
        out_specs=(tokens, tokens, grads, grads, grads),
        check_vma=False,
    )
```

```python
import functools

import jax
import jax.numpy as jnp
from jax import lax
from jax.experimental import pallas as pl
from jax.experimental.pallas import tpu as pltpu
from jax.sharding import PartitionSpec as P

F32 = jnp.float32
BF16 = jnp.bfloat16
LANE = 128


def dot(a, b, dims):
    return lax.dot_general(a, b, (dims, ((), ())), preferred_element_type=F32)


def routing(routes, probs, experts):
    tok, top = routes.shape
    picks = routes[:, :, None] == jnp.arange(experts, dtype=jnp.int32)[None, None, :]
    chosen = jnp.any(picks, axis=1)
    weight = jnp.sum(jnp.where(picks, probs[:, :, None], 0.0), axis=1)
    order = jnp.arange(tok, dtype=jnp.int32)
    earlier = (order[:, None] > order[None, :]).astype(BF16)
    place = dot(earlier, chosen.astype(BF16), ((1,), (0,))).astype(jnp.int32)
    place = jnp.where(chosen, place, -1)
    return picks, place, weight


def general(hidden_in, out_grad, routes, probs, w_gate, w_up, w_down):
    tok, top = routes.shape
    width = hidden_in.shape[1]
    ep = lax.axis_size("ep")
    experts = ep * w_gate.shape[0]
    cap = max(8, 2 * tok * top // experts)
    rows = experts * cap
    picks, place, weight = routing(routes, probs, experts)
    slot = jnp.arange(cap, dtype=jnp.int32)
    select = place.T[:, None, :] == slot[None, :, None]
    select_rows = select.reshape(rows, tok).astype(BF16)
    row_weight = jnp.sum(jnp.where(select, weight.T[:, None, :], 0.0), axis=2).reshape(rows, 1)
    send_in = dot(select_rows, hidden_in, ((1,), (0,))).astype(BF16)
    send_grad = dot(select_rows, out_grad, ((1,), (0,))).astype(BF16)
    send_grad = jnp.concatenate(
        [send_grad, jnp.broadcast_to(row_weight.astype(BF16), (rows, LANE))], axis=1
    )

    def swap(value):
        return lax.all_to_all(
            value.reshape(experts, cap, -1), "ep", split_axis=0, concat_axis=0, tiled=True
        ).reshape(rows, -1)

    gate_full, up_full, down_full = (
        lax.all_gather(w[0], "edp", axis=0, tiled=True) for w in (w_gate, w_up, w_down)
    )
    rows_in = swap(send_in)
    got = swap(send_grad)
    rows_grad = got[:, :width]
    p = got[:, width : width + 1].astype(F32)
    gate = dot(rows_in, gate_full, ((1,), (0,)))
    upper = dot(rows_in, up_full, ((1,), (0,)))
    sigma = jax.nn.sigmoid(gate)
    active = gate * sigma
    hidden = active * upper
    plain = dot(rows_grad, down_full, ((1,), (1,)))
    prob_grad = jnp.sum(hidden * plain, axis=1, keepdims=True)
    hidden_grad = plain * p
    up_grad = (hidden_grad * active).astype(BF16)
    gate_grad = (hidden_grad * upper * sigma * (1.0 + gate * (1.0 - sigma))).astype(BF16)
    scaled_hidden = (hidden * p).astype(BF16)
    row_grad = dot(gate_grad, gate_full, ((1,), (1,))) + dot(up_grad, up_full, ((1,), (1,)))
    row_grad = jnp.concatenate(
        [row_grad.astype(BF16), jnp.broadcast_to(prob_grad.astype(BF16), (rows, LANE))], axis=1
    )
    row_grad, gate_grad, up_grad, scaled_hidden = lax.optimization_barrier(
        (row_grad, gate_grad, up_grad, scaled_hidden)
    )
    back = swap(row_grad)
    input_grad = dot(select_rows, back[:, :width], ((0,), (0,))).astype(BF16)
    back_prob = back[:, width].astype(F32).reshape(experts, cap, 1)
    by_expert = jnp.sum(jnp.where(select, back_prob, 0.0), axis=1).T
    prob_out = jnp.sum(jnp.where(picks, by_expert[:, None, :], 0.0), axis=2)

    def share(a, b):
        term = dot(a, b, ((0,), (0,))).astype(BF16)
        return lax.psum_scatter(term, "edp", scatter_dimension=0, tiled=True)[None]

    return (
        input_grad,
        prob_out,
        share(rows_in, gate_grad),
        share(rows_in, up_grad),
        share(scaled_hidden, rows_grad),
    )


def partner(me, bits, d):
    total = 0
    for i in range(bits):
        bit = lax.rem(me // (1 << i), 2)
        total = total + (1 - bit if (d >> i) & 1 else bit) * (1 << i)
    return total


def kernel(ep, piece, hidden, grad, select, select_t, weight, wg, wu, wd,
           in_out, prob_out, gw, uw, dw,
           send_in, send_grad, rows_in, rows_grad, send_back, back,
           gate_full, up_full, down_full, active, upper, slope,
           gate_grad, up_grad, scaled, gate_send, up_send, down_send,
           gate_got, up_got, down_got,
           row_send, row_recv, own_sem, w_send, w_recv, w_own, g_send, g_recv):
    me, side = lax.axis_index("ep"), lax.axis_index("edp")
    other = 1 - side
    bits = ep.bit_length() - 1
    width, ff = hidden.shape[1], wg.shape[1]
    part_rows = ep * piece
    half, down_half = width // 2, ff // 2
    partners = [(d, partner(me, bits, d)) for d in range(ep - 1, 0, -1)]

    barrier = pltpu.get_barrier_semaphore()
    for d, target in partners:
        pl.semaphore_signal(barrier, inc=1, device_id={"ep": target})
    pl.semaphore_signal(barrier, inc=1, device_id={"edp": other})

    def row_slice(part, owner):
        return pl.ds(pl.multiple_of(part * part_rows + owner * piece, piece), piece)

    def dispatch(part, source, sink):
        rows = pl.ds(part * part_rows, part_rows)

        def tile(c, carry):
            cols = pl.ds(pl.multiple_of(c * 512, 512), 512)
            sink[rows, cols] = dot(select[rows, :], source[:, cols], ((1,), (0,))).astype(BF16)
            return carry

        lax.fori_loop(0, width // 512, tile, 0)

    def spread(kind, part, source, sink):
        copies = []
        for d, target in partners:
            copies.append(pltpu.make_async_remote_copy(
                src_ref=source.at[row_slice(part, target)],
                dst_ref=sink.at[row_slice(part, me)],
                send_sem=row_send.at[kind, part, d],
                recv_sem=row_recv.at[kind, part, d],
                device_id={"ep": target},
            ))
        for copy in copies:
            copy.start()
        own = pltpu.make_async_copy(
            source.at[row_slice(part, me)], sink.at[row_slice(part, me)], own_sem.at[kind, part])
        own.start()
        return copies, own

    def arrive(group):
        copies, own = group
        own.wait()
        for copy in copies:
            copy.wait_recv()

    dispatch(0, hidden, send_in)
    pl.semaphore_wait(barrier, ep)
    in0 = spread(0, 0, send_in, rows_in)
    dispatch(0, grad, send_grad)
    send_grad[:, pl.ds(width, LANE)] = weight[...]
    grad0 = spread(1, 0, send_grad, rows_grad)

    exchanged = []
    for i, (ref, full) in enumerate(((wg, gate_full), (wu, up_full), (wd, down_full))):
        depth = ref.shape[0]
        place = pl.ds(pl.multiple_of(side * depth, depth), depth)
        copy = pltpu.make_async_remote_copy(
            src_ref=ref, dst_ref=full.at[place], send_sem=w_send.at[i], recv_sem=w_recv.at[i],
            device_id={"edp": other})
        copy.start()
        own = pltpu.make_async_copy(ref, full.at[place], w_own.at[i])
        own.start()
        exchanged.append((copy, own))

    dispatch(1, hidden, send_in)
    in1 = spread(0, 1, send_in, rows_in)
    dispatch(1, grad, send_grad)
    grad1 = spread(1, 1, send_grad, rows_grad)

    for copy, own in exchanged:
        own.wait()
        copy.wait_recv()

    def forward(part):
        rows = pl.ds(part * part_rows, part_rows)

        def tile(c, carry):
            cols = pl.ds(pl.multiple_of(c * 256, 256), 256)
            x = rows_in[rows, :]
            gate = dot(x, gate_full[:, cols], ((1,), (0,)))
            up = dot(x, up_full[:, cols], ((1,), (0,)))
            sigma = jax.nn.sigmoid(gate)
            active[:, cols] = gate * sigma
            upper[:, cols] = up
            slope[:, cols] = up * sigma * (1.0 + gate * (1.0 - sigma))
            return carry

        lax.fori_loop(0, ff // 256, tile, 0)

    def backward(part):
        rows = pl.ds(part * part_rows, part_rows)
        p = rows_grad[rows, pl.ds(width, LANE)].astype(F32)[:, :1]

        def tile(c, total):
            cols = pl.ds(pl.multiple_of(c * 256, 256), 256)
            plain = dot(rows_grad[rows, pl.ds(0, width)], down_full[cols, :], ((1,), (1,)))
            act = active[:, cols]
            hid = act * upper[:, cols]
            hidden_grad = plain * p
            up_grad[rows, cols] = (hidden_grad * act).astype(BF16)
            gate_grad[rows, cols] = (hidden_grad * slope[:, cols]).astype(BF16)
            scaled[rows, cols] = (hid * p).astype(BF16)
            return total + jnp.sum(hid * plain, axis=1, keepdims=True)

        total = lax.fori_loop(0, ff // 256, tile, jnp.zeros((part_rows, 1), F32))
        send_back[rows, pl.ds(width, LANE)] = jnp.broadcast_to(total, (part_rows, LANE)).astype(BF16)

        def out_tile(c, carry):
            cols = pl.ds(pl.multiple_of(c * 256, 256), 256)
            value = dot(gate_grad[rows, :], gate_full[cols, :], ((1,), (1,)))
            value = value + dot(up_grad[rows, :], up_full[cols, :], ((1,), (1,)))
            send_back[rows, cols] = value.astype(BF16)
            return carry

        lax.fori_loop(0, width // 256, out_tile, 0)

    arrive(in0)
    forward(0)
    arrive(grad0)
    backward(0)
    back0 = spread(2, 0, send_back, back)
    arrive(in1)
    forward(1)
    arrive(grad1)
    backward(1)
    back1 = spread(2, 1, send_back, back)

    def wide(which, sink, factor):
        def tile(c, carry):
            at = pl.ds(pl.multiple_of(which * half + c * 256, 256), 256)
            value = dot(rows_in[:, at], factor[...], ((0,), (0,)))
            sink[pl.ds(pl.multiple_of(c * 256, 256), 256), :] = value.astype(BF16)
            return carry

        lax.fori_loop(0, half // 256, tile, 0)

    def tall(which, sink):
        lhs = pl.ds(pl.multiple_of(which * down_half, LANE), down_half)

        def tile(c, carry):
            cols = pl.ds(pl.multiple_of(c * 512, 512), 512)
            sink[:, cols] = dot(scaled[:, lhs], rows_grad[:, cols], ((0,), (0,))).astype(BF16)
            return carry

        lax.fori_loop(0, width // 512, tile, 0)

    def pass_on(i, source, sink):
        copy = pltpu.make_async_remote_copy(
            src_ref=source, dst_ref=sink, send_sem=g_send.at[i], recv_sem=g_recv.at[i],
            device_id={"edp": other})
        copy.start()
        return copy

    wide(other, gate_send, gate_grad)
    passed = [pass_on(0, gate_send, gate_got)]
    wide(other, up_send, up_grad)
    passed.append(pass_on(1, up_send, up_got))
    tall(other, down_send)
    passed.append(pass_on(2, down_send, down_got))
    wide(side, gw, gate_grad)
    wide(side, uw, up_grad)
    tall(side, dw)
    for copy, got, sink in zip(passed, (gate_got, up_got, down_got), (gw, uw, dw)):
        copy.wait_recv()
        steps = sink.shape[0] // 128

        def add(r, carry, got=got, sink=sink):
            at = pl.ds(pl.multiple_of(r * 128, 128), 128)
            sink[at, :] = (sink[at, :].astype(F32) + got[at, :].astype(F32)).astype(BF16)
            return carry

        lax.fori_loop(0, steps, add, 0)

    arrive(back0)
    arrive(back1)

    def combine(c, carry):
        cols = pl.ds(pl.multiple_of(c * 512, 512), 512)
        in_out[:, cols] = dot(select_t[...], back[:, cols], ((1,), (0,))).astype(BF16)
        return carry

    lax.fori_loop(0, width // 512, combine, 0)
    prob_out[...] = back[:, pl.ds(width, LANE)]
    for copies, own in (in0, grad0, in1, grad1, back0, back1):
        for copy in copies:
            copy.wait_send()
    for copy, own in exchanged:
        copy.wait_send()
    for copy in passed:
        copy.wait_send()


def fused(hidden_in, out_grad, routes, probs, w_gate, w_up, w_down):
    tok, top = routes.shape
    width = hidden_in.shape[1]
    ep = lax.axis_size("ep")
    ff = w_gate.shape[2]
    cap = 2 * tok * top // ep
    piece = cap // 2
    rows = ep * cap
    picks, place, weight = routing(routes, probs, ep)
    slot = jnp.arange(cap, dtype=jnp.int32).reshape(2, 1, piece, 1)
    select = place.T[None, :, None, :] == slot
    row_weight = jnp.sum(jnp.where(select, weight.T[None, :, None, :], 0.0), axis=3)
    row_weight = jnp.broadcast_to(row_weight.reshape(rows, 1).astype(BF16), (rows, LANE))
    select_rows = select.reshape(rows, tok).astype(BF16)
    vmem = pl.BlockSpec(memory_space=pltpu.VMEM)
    hbm = pl.BlockSpec(memory_space=pl.ANY)

    def buf(*shape, dtype=BF16):
        return pltpu.VMEM(shape, dtype)

    wide, down = (width // 2, ff), (ff // 2, width)
    dma = pltpu.SemaphoreType.DMA
    input_grad, back_prob, gw, uw, dw = pl.pallas_call(
        functools.partial(kernel, ep, piece),
        out_shape=(
            jax.ShapeDtypeStruct((tok, width), BF16),
            jax.ShapeDtypeStruct((rows, LANE), BF16),
            jax.ShapeDtypeStruct(wide, BF16),
            jax.ShapeDtypeStruct(wide, BF16),
            jax.ShapeDtypeStruct(down, BF16),
        ),
        in_specs=[vmem] * 5 + [hbm] * 3,
        out_specs=(vmem,) * 5,
        scratch_shapes=[
            buf(rows, width), buf(rows, width + LANE), buf(rows, width), buf(rows, width + LANE),
            buf(rows, width + LANE), buf(rows, width + LANE),
            buf(width, ff), buf(width, ff), buf(ff, width),
            buf(rows // 2, ff, dtype=F32), buf(rows // 2, ff, dtype=F32), buf(rows // 2, ff, dtype=F32),
            buf(rows, ff), buf(rows, ff), buf(rows, ff),
            buf(*wide), buf(*wide), buf(*down), buf(*wide), buf(*wide), buf(*down),
            dma((3, 2, ep)), dma((3, 2, ep)), dma((3, 2)),
            dma((3,)), dma((3,)), dma((3,)), dma((3,)), dma((3,)),
        ],
        compiler_params=pltpu.CompilerParams(
            collective_id=0, has_side_effects=True, vmem_limit_bytes=60 << 20
        ),
        cost_estimate=pl.CostEstimate(
            flops=16 * rows * width * ff, bytes_accessed=24 * rows * width, transcendentals=rows * ff
        ),
    )(hidden_in, out_grad, select_rows, select_rows.T, row_weight, w_gate[0], w_up[0], w_down[0])
    back_prob = back_prob[:, 0].astype(F32).reshape(2, ep, piece, 1)
    by_expert = jnp.sum(jnp.where(select, back_prob, 0.0), axis=(0, 2)).T
    prob_grad = jnp.sum(jnp.where(picks, by_expert[:, None, :], 0.0), axis=2)
    return input_grad, prob_grad, gw[None], uw[None], dw[None]


def local(*arrays):
    tok, top = arrays[2].shape
    width, ff = arrays[4].shape[1] * 2, arrays[4].shape[2]
    ep = lax.axis_size("ep")
    whole_tiles = tok % 128 == 0 and width % 512 == 0 and ff % 256 == 0
    one_each = arrays[4].shape[0] == 1 and lax.axis_size("edp") == 2
    if one_each and whole_tiles and ep <= 8 and ep & (ep - 1) == 0 and 2 * tok * top // ep % 64 == 0:
        return fused(*arrays)
    return general(*arrays)


def solution(mesh):
    tokens = P(("groups", "ep", "edp"), None)
    weights = P("ep", "edp", None)
    grads = P(("groups", "ep"), "edp", None)
    return jax.shard_map(
        local,
        mesh=mesh,
        in_specs=(tokens,) * 4 + (weights,) * 3,
        out_specs=(tokens, tokens, grads, grads, grads),
        check_vma=False,
    )
```

```python
import functools

import jax
import jax.numpy as jnp
from jax import lax
from jax.experimental import pallas as pl
from jax.experimental.pallas import tpu as pltpu
from jax.sharding import PartitionSpec as P

F32 = jnp.float32
BF16 = jnp.bfloat16
LANE = 128


def dot(a, b, dims):
    return lax.dot_general(a, b, (dims, ((), ())), preferred_element_type=F32)


def routing(routes, probs, experts):
    tok, top = routes.shape
    picks = routes[:, :, None] == jnp.arange(experts, dtype=jnp.int32)[None, None, :]
    chosen = jnp.any(picks, axis=1)
    weight = jnp.sum(jnp.where(picks, probs[:, :, None], 0.0), axis=1)
    order = jnp.arange(tok, dtype=jnp.int32)
    earlier = (order[:, None] > order[None, :]).astype(BF16)
    place = dot(earlier, chosen.astype(BF16), ((1,), (0,))).astype(jnp.int32)
    place = jnp.where(chosen, place, -1)
    return picks, place, weight


def general(hidden_in, out_grad, routes, probs, w_gate, w_up, w_down):
    tok, top = routes.shape
    width = hidden_in.shape[1]
    ep = lax.axis_size("ep")
    experts = ep * w_gate.shape[0]
    cap = max(8, 2 * tok * top // experts)
    rows = experts * cap
    picks, place, weight = routing(routes, probs, experts)
    slot = jnp.arange(cap, dtype=jnp.int32)
    select = place.T[:, None, :] == slot[None, :, None]
    select_rows = select.reshape(rows, tok).astype(BF16)
    row_weight = jnp.sum(jnp.where(select, weight.T[:, None, :], 0.0), axis=2).reshape(rows, 1)
    send_in = dot(select_rows, hidden_in, ((1,), (0,))).astype(BF16)
    send_grad = dot(select_rows, out_grad, ((1,), (0,))).astype(BF16)
    send_grad = jnp.concatenate(
        [send_grad, jnp.broadcast_to(row_weight.astype(BF16), (rows, LANE))], axis=1
    )

    def swap(value):
        return lax.all_to_all(
            value.reshape(experts, cap, -1), "ep", split_axis=0, concat_axis=0, tiled=True
        ).reshape(rows, -1)

    gate_full, up_full, down_full = (
        lax.all_gather(w[0], "edp", axis=0, tiled=True) for w in (w_gate, w_up, w_down)
    )
    rows_in = swap(send_in)
    got = swap(send_grad)
    rows_grad = got[:, :width]
    p = got[:, width : width + 1].astype(F32)
    gate = dot(rows_in, gate_full, ((1,), (0,)))
    upper = dot(rows_in, up_full, ((1,), (0,)))
    sigma = jax.nn.sigmoid(gate)
    active = gate * sigma
    hidden = active * upper
    plain = dot(rows_grad, down_full, ((1,), (1,)))
    prob_grad = jnp.sum(hidden * plain, axis=1, keepdims=True)
    hidden_grad = plain * p
    up_grad = (hidden_grad * active).astype(BF16)
    gate_grad = (hidden_grad * upper * sigma * (1.0 + gate * (1.0 - sigma))).astype(BF16)
    scaled_hidden = (hidden * p).astype(BF16)
    row_grad = dot(gate_grad, gate_full, ((1,), (1,))) + dot(up_grad, up_full, ((1,), (1,)))
    row_grad = jnp.concatenate(
        [row_grad.astype(BF16), jnp.broadcast_to(prob_grad.astype(BF16), (rows, LANE))], axis=1
    )
    row_grad, gate_grad, up_grad, scaled_hidden = lax.optimization_barrier(
        (row_grad, gate_grad, up_grad, scaled_hidden)
    )
    back = swap(row_grad)
    input_grad = dot(select_rows, back[:, :width], ((0,), (0,))).astype(BF16)
    back_prob = back[:, width].astype(F32).reshape(experts, cap, 1)
    by_expert = jnp.sum(jnp.where(select, back_prob, 0.0), axis=1).T
    prob_out = jnp.sum(jnp.where(picks, by_expert[:, None, :], 0.0), axis=2)

    def share(a, b):
        term = dot(a, b, ((0,), (0,))).astype(BF16)
        return lax.psum_scatter(term, "edp", scatter_dimension=0, tiled=True)[None]

    return (
        input_grad,
        prob_out,
        share(rows_in, gate_grad),
        share(rows_in, up_grad),
        share(scaled_hidden, rows_grad),
    )


def partner(me, bits, d):
    total = 0
    for i in range(bits):
        bit = lax.rem(me // (1 << i), 2)
        total = total + (1 - bit if (d >> i) & 1 else bit) * (1 << i)
    return total


def kernel(quad, cap, hidden, grad, table, wg, wu, wd,
           in_out, prob_out, gw, uw, dw,
           send_in, send_grad, rows_in, rows_grad, send_back, back,
           gate_full, up_full, down_full, active, upper, slope,
           gate_grad, up_grad, scaled, gate_send, up_send, down_send,
           gate_got, up_got, down_got,
           far_table, far_hidden, far_grad, select, relay_in, far_in, relay_prob, far_prob,
           row_send, row_recv, own_sem, w_send, w_recv, w_own, g_send, g_recv, m_send, m_recv):
    me, side = lax.axis_index("ep"), lax.axis_index("edp")
    other = 1 - side
    team, seat = me // quad, lax.rem(me, quad)
    mirror = (1 - team) * quad + seat
    bits = quad.bit_length() - 1
    width, ff = hidden.shape[1], wg.shape[1]
    tok = hidden.shape[0]
    part_rows = quad * cap
    half, down_half = width // 2, ff // 2
    partners = [(d, partner(seat, bits, d)) for d in range(quad - 1, 0, -1)]

    barrier = pltpu.get_barrier_semaphore()
    for d, target in partners:
        pl.semaphore_signal(barrier, inc=1, device_id={"ep": team * quad + target})
    pl.semaphore_signal(barrier, inc=1, device_id={"ep": mirror})
    pl.semaphore_signal(barrier, inc=1, device_id={"edp": other})

    def row_slice(part, owner):
        return pl.ds(pl.multiple_of(part * part_rows + owner * cap, cap), cap)

    def choose(part, entry):
        slot = lax.broadcasted_iota(jnp.int32, (cap, tok), 0).astype(F32)
        for q in range(quad):
            rows = pl.ds(part * part_rows + q * cap, cap)
            mask = entry[q : q + 1, :] == slot
            select[rows, :] = jnp.where(mask, 1.0, 0.0).astype(BF16)
            w = jnp.sum(jnp.where(mask, entry[quad + q : quad + q + 1, :], 0.0), axis=1, keepdims=True)
            send_grad[rows, pl.ds(width, LANE)] = jnp.broadcast_to(w, (cap, LANE)).astype(BF16)

    def dispatch(part, source, sink):
        rows = pl.ds(part * part_rows, part_rows)

        def tile(c, carry):
            cols = pl.ds(pl.multiple_of(c * 512, 512), 512)
            sink[rows, cols] = dot(select[rows, :], source[:, cols], ((1,), (0,))).astype(BF16)
            return carry

        lax.fori_loop(0, width // 512, tile, 0)

    def spread(kind, part, source, sink, low, size):
        cols = pl.ds(low, size)
        copies = []
        for d, target in partners:
            copies.append(pltpu.make_async_remote_copy(
                src_ref=source.at[row_slice(part, target), cols],
                dst_ref=sink.at[row_slice(part, seat), cols],
                send_sem=row_send.at[kind, part, d],
                recv_sem=row_recv.at[kind, part, d],
                device_id={"ep": team * quad + target},
            ))
        for copy in copies:
            copy.start()
        own = pltpu.make_async_copy(
            source.at[row_slice(part, seat), cols], sink.at[row_slice(part, seat), cols],
            own_sem.at[kind, part])
        own.start()
        return copies, own

    def arrive(group):
        copies, own = group
        own.wait()
        for copy in copies:
            copy.wait_recv()

    def cross(i, source, sink):
        copy = pltpu.make_async_remote_copy(
            src_ref=source, dst_ref=sink, send_sem=m_send.at[i], recv_sem=m_recv.at[i],
            device_id={"ep": mirror})
        copy.start()
        return copy

    choose(0, table[team])
    dispatch(0, hidden, send_in)
    pl.semaphore_wait(barrier, quad + 1)
    crossed = [cross(0, table.at[1 - team], far_table), cross(1, hidden, far_hidden)]
    in0 = spread(0, 0, send_in, rows_in, 0, width)
    crossed.append(cross(2, grad, far_grad))
    dispatch(0, grad, send_grad)
    grad0 = spread(1, 0, send_grad, rows_grad, 0, width + LANE)

    exchanged = []
    for i, (ref, full) in enumerate(((wg, gate_full), (wu, up_full), (wd, down_full))):
        depth = ref.shape[0]
        place = pl.ds(pl.multiple_of(side * depth, depth), depth)
        copy = pltpu.make_async_remote_copy(
            src_ref=ref, dst_ref=full.at[place], send_sem=w_send.at[i], recv_sem=w_recv.at[i],
            device_id={"edp": other})
        copy.start()
        own = pltpu.make_async_copy(ref, full.at[place], w_own.at[i])
        own.start()
        exchanged.append((copy, own))

    crossed[0].wait_recv()
    choose(1, far_table[...])
    crossed[1].wait_recv()
    dispatch(1, far_hidden, send_in)
    in1 = spread(0, 1, send_in, rows_in, 0, width)
    for copy, own in exchanged:
        own.wait()
        copy.wait_recv()

    def forward(part):
        rows = pl.ds(part * part_rows, part_rows)

        def tile(c, carry):
            cols = pl.ds(pl.multiple_of(c * 256, 256), 256)
            x = rows_in[rows, :]
            gate = dot(x, gate_full[:, cols], ((1,), (0,)))
            up = dot(x, up_full[:, cols], ((1,), (0,)))
            sigma = jax.nn.sigmoid(gate)
            active[:, cols] = gate * sigma
            upper[:, cols] = up
            slope[:, cols] = up * sigma * (1.0 + gate * (1.0 - sigma))
            return carry

        lax.fori_loop(0, ff // 256, tile, 0)

    def backward(part):
        rows = pl.ds(part * part_rows, part_rows)
        p = rows_grad[rows, pl.ds(width, LANE)].astype(F32)[:, :1]

        def tile(c, total):
            cols = pl.ds(pl.multiple_of(c * 256, 256), 256)
            plain = dot(rows_grad[rows, pl.ds(0, width)], down_full[cols, :], ((1,), (1,)))
            act = active[:, cols]
            hid = act * upper[:, cols]
            hidden_grad = plain * p
            up_grad[rows, cols] = (hidden_grad * act).astype(BF16)
            gate_grad[rows, cols] = (hidden_grad * slope[:, cols]).astype(BF16)
            scaled[rows, cols] = (hid * p).astype(BF16)
            return total + jnp.sum(hid * plain, axis=1, keepdims=True)

        total = lax.fori_loop(0, ff // 256, tile, jnp.zeros((part_rows, 1), F32))
        send_back[rows, pl.ds(width, LANE)] = jnp.broadcast_to(total, (part_rows, LANE)).astype(BF16)

    def returns(part, kind, low, size):
        rows = pl.ds(part * part_rows, part_rows)

        def out_tile(c, carry):
            cols = pl.ds(pl.multiple_of(c * 256, 256), 256)
            value = dot(gate_grad[rows, :], gate_full[cols, :], ((1,), (1,)))
            value = value + dot(up_grad[rows, :], up_full[cols, :], ((1,), (1,)))
            send_back[rows, cols] = value.astype(BF16)
            return carry

        lax.fori_loop(low // 256, (low + size) // 256, out_tile, 0)
        tail = LANE if low + size == width else 0
        return spread(kind, part, send_back, back, low, size + tail)

    arrive(in0)
    forward(0)
    crossed[2].wait_recv()
    dispatch(1, far_grad, send_grad)
    grad1 = spread(1, 1, send_grad, rows_grad, 0, width + LANE)
    arrive(grad0)
    backward(0)
    back0 = returns(0, 2, 0, width)
    arrive(in1)
    forward(1)
    arrive(grad1)
    backward(1)
    back1 = [returns(1, 2, 0, half), returns(1, 3, half, half)]

    def wide(which, sink, factor):
        def tile(c, carry):
            at = pl.ds(pl.multiple_of(which * half + c * 256, 256), 256)
            value = dot(rows_in[:, at], factor[...], ((0,), (0,)))
            sink[pl.ds(pl.multiple_of(c * 256, 256), 256), :] = value.astype(BF16)
            return carry

        lax.fori_loop(0, half // 256, tile, 0)

    def tall(which, sink):
        lhs = pl.ds(pl.multiple_of(which * down_half, LANE), down_half)

        def tile(c, carry):
            cols = pl.ds(pl.multiple_of(c * 512, 512), 512)
            sink[:, cols] = dot(scaled[:, lhs], rows_grad[:, cols], ((0,), (0,))).astype(BF16)
            return carry

        lax.fori_loop(0, width // 512, tile, 0)

    def pass_on(i, source, sink):
        copy = pltpu.make_async_remote_copy(
            src_ref=source, dst_ref=sink, send_sem=g_send.at[i], recv_sem=g_recv.at[i],
            device_id={"edp": other})
        copy.start()
        return copy

    wide(other, gate_send, gate_grad)
    passed = [pass_on(0, gate_send, gate_got)]
    wide(other, up_send, up_grad)
    passed.append(pass_on(1, up_send, up_got))
    tall(other, down_send)
    passed.append(pass_on(2, down_send, down_got))

    def combine(part, sink, low, size, extra=None):
        rows = pl.ds(part * part_rows, part_rows)

        def tile(c, carry):
            cols = pl.ds(pl.multiple_of(c * 512, 512), 512)
            value = dot(select[rows, :], back[rows, cols], ((0,), (0,)))
            if extra is not None:
                value = value + extra[:, cols].astype(F32)
            sink[:, cols] = value.astype(BF16)
            return carry

        lax.fori_loop(low // 512, (low + size) // 512, tile, 0)

    def prob_table(part):
        lines = []
        for q in range(quad):
            rows = pl.ds(part * part_rows + q * cap, cap)
            value = select[rows, :].astype(F32) * back[rows, pl.ds(width, LANE)].astype(F32)
            lines.append(jnp.sum(value, axis=0, keepdims=True))
        return jnp.concatenate(lines + lines, axis=0)

    for i, group in enumerate(back1):
        arrive(group)
        combine(1, relay_in, i * half, half)
        cols = pl.ds(i * half, half)
        crossed.append(cross(3 + i, relay_in.at[:, cols], far_in.at[:, cols]))
    relay_prob[...] = prob_table(1)
    crossed.append(cross(5, relay_prob, far_prob))
    wide(side, gw, gate_grad)
    wide(side, uw, up_grad)
    tall(side, dw)
    for copy, got, sink in zip(passed, (gate_got, up_got, down_got), (gw, uw, dw)):
        copy.wait_recv()
        steps = sink.shape[0] // 128

        def add(r, carry, got=got, sink=sink):
            at = pl.ds(pl.multiple_of(r * 128, 128), 128)
            sink[at, :] = (sink[at, :].astype(F32) + got[at, :].astype(F32)).astype(BF16)
            return carry

        lax.fori_loop(0, steps, add, 0)

    arrive(back0)
    prob_out[team] = prob_table(0)
    for i in range(2):
        crossed[3 + i].wait_recv()
        combine(0, in_out, i * half, half, far_in)
    crossed[5].wait_recv()
    prob_out[1 - team] = far_prob[...]
    for copies, own in (in0, grad0, in1, grad1, back0, back1[0], back1[1]):
        for copy in copies:
            copy.wait_send()
    for copy in crossed:
        copy.wait_send()
    for copy, own in exchanged:
        copy.wait_send()
    for copy in passed:
        copy.wait_send()


def fused(hidden_in, out_grad, routes, probs, w_gate, w_up, w_down):
    tok, top = routes.shape
    width = hidden_in.shape[1]
    ep = lax.axis_size("ep")
    ff = w_gate.shape[2]
    cap = 2 * tok * top // ep
    quad = ep // 2
    rows = ep * cap
    picks, place, weight = routing(routes, probs, ep)
    table = jnp.concatenate(
        [place.T.astype(F32).reshape(2, quad, tok), weight.T.reshape(2, quad, tok)], axis=1
    )
    vmem = pl.BlockSpec(memory_space=pltpu.VMEM)
    hbm = pl.BlockSpec(memory_space=pl.ANY)

    def buf(*shape, dtype=BF16):
        return pltpu.VMEM(shape, dtype)

    wide, down = (width // 2, ff), (ff // 2, width)
    dma = pltpu.SemaphoreType.DMA
    input_grad, back_prob, gw, uw, dw = pl.pallas_call(
        functools.partial(kernel, quad, cap),
        out_shape=(
            jax.ShapeDtypeStruct((tok, width), BF16),
            jax.ShapeDtypeStruct((2, ep, tok), F32),
            jax.ShapeDtypeStruct(wide, BF16),
            jax.ShapeDtypeStruct(wide, BF16),
            jax.ShapeDtypeStruct(down, BF16),
        ),
        in_specs=[vmem] * 3 + [hbm] * 3,
        out_specs=(vmem,) * 5,
        scratch_shapes=[
            buf(rows, width), buf(rows, width + LANE), buf(rows, width), buf(rows, width + LANE),
            buf(rows, width + LANE), buf(rows, width + LANE),
            buf(width, ff), buf(width, ff), buf(ff, width),
            buf(rows // 2, ff, dtype=F32), buf(rows // 2, ff, dtype=F32), buf(rows // 2, ff, dtype=F32),
            buf(rows, ff), buf(rows, ff), buf(rows, ff),
            buf(*wide), buf(*wide), buf(*down), buf(*wide), buf(*wide), buf(*down),
            buf(ep, tok, dtype=F32), buf(tok, width), buf(tok, width), buf(rows, tok),
            buf(tok, width), buf(tok, width), buf(ep, tok, dtype=F32), buf(ep, tok, dtype=F32),
            dma((4, 2, quad)), dma((4, 2, quad)), dma((4, 2)),
            dma((3,)), dma((3,)), dma((3,)), dma((3,)), dma((3,)), dma((6,)), dma((6,)),
        ],
        compiler_params=pltpu.CompilerParams(
            collective_id=0, has_side_effects=True, vmem_limit_bytes=60 << 20
        ),
        cost_estimate=pl.CostEstimate(
            flops=16 * rows * width * ff, bytes_accessed=24 * rows * width, transcendentals=rows * ff
        ),
    )(hidden_in, out_grad, table, w_gate[0], w_up[0], w_down[0])
    by_expert = back_prob[:, :quad].reshape(ep, tok).T
    prob_grad = jnp.sum(jnp.where(picks, by_expert[:, None, :], 0.0), axis=2)
    return input_grad, prob_grad, gw[None], uw[None], dw[None]


def local(*arrays):
    tok, top = arrays[2].shape
    width, ff = arrays[4].shape[1] * 2, arrays[4].shape[2]
    ep = lax.axis_size("ep")
    whole_tiles = tok % 128 == 0 and width % 512 == 0 and ff % 256 == 0
    one_each = arrays[4].shape[0] == 1 and lax.axis_size("edp") == 2
    if one_each and whole_tiles and ep == 8 and tok == LANE and 2 * tok * top // ep % 32 == 0:
        return fused(*arrays)
    return general(*arrays)


def solution(mesh):
    tokens = P(("groups", "ep", "edp"), None)
    weights = P("ep", "edp", None)
    grads = P(("groups", "ep"), "edp", None)
    return jax.shard_map(
        local,
        mesh=mesh,
        in_specs=(tokens,) * 4 + (weights,) * 3,
        out_specs=(tokens, tokens, grads, grads, grads),
        check_vma=False,
    )
```

```python
import functools

import jax
import jax.numpy as jnp
from jax import lax
from jax.experimental import pallas as pl
from jax.experimental.pallas import tpu as pltpu
from jax.sharding import PartitionSpec as P

F32 = jnp.float32
BF16 = jnp.bfloat16
LANE = 128


def dot(a, b, dims):
    return lax.dot_general(a, b, (dims, ((), ())), preferred_element_type=F32)


def routing(routes, probs, experts):
    tok, top = routes.shape
    picks = routes[:, :, None] == jnp.arange(experts, dtype=jnp.int32)[None, None, :]
    chosen = jnp.any(picks, axis=1)
    weight = jnp.sum(jnp.where(picks, probs[:, :, None], 0.0), axis=1)
    order = jnp.arange(tok, dtype=jnp.int32)
    earlier = (order[:, None] > order[None, :]).astype(BF16)
    place = dot(earlier, chosen.astype(BF16), ((1,), (0,))).astype(jnp.int32)
    place = jnp.where(chosen, place, -1)
    return picks, place, weight


def general(hidden_in, out_grad, routes, probs, w_gate, w_up, w_down):
    tok, top = routes.shape
    width = hidden_in.shape[1]
    ep = lax.axis_size("ep")
    experts = ep * w_gate.shape[0]
    cap = max(8, 2 * tok * top // experts)
    rows = experts * cap
    picks, place, weight = routing(routes, probs, experts)
    slot = jnp.arange(cap, dtype=jnp.int32)
    select = place.T[:, None, :] == slot[None, :, None]
    select_rows = select.reshape(rows, tok).astype(BF16)
    row_weight = jnp.sum(jnp.where(select, weight.T[:, None, :], 0.0), axis=2).reshape(rows, 1)
    send_in = dot(select_rows, hidden_in, ((1,), (0,))).astype(BF16)
    send_grad = dot(select_rows, out_grad, ((1,), (0,))).astype(BF16)
    send_grad = jnp.concatenate(
        [send_grad, jnp.broadcast_to(row_weight.astype(BF16), (rows, LANE))], axis=1
    )

    def swap(value):
        return lax.all_to_all(
            value.reshape(experts, cap, -1), "ep", split_axis=0, concat_axis=0, tiled=True
        ).reshape(rows, -1)

    gate_full, up_full, down_full = (
        lax.all_gather(w[0], "edp", axis=0, tiled=True) for w in (w_gate, w_up, w_down)
    )
    rows_in = swap(send_in)
    got = swap(send_grad)
    rows_grad = got[:, :width]
    p = got[:, width : width + 1].astype(F32)
    gate = dot(rows_in, gate_full, ((1,), (0,)))
    upper = dot(rows_in, up_full, ((1,), (0,)))
    sigma = jax.nn.sigmoid(gate)
    active = gate * sigma
    hidden = active * upper
    plain = dot(rows_grad, down_full, ((1,), (1,)))
    prob_grad = jnp.sum(hidden * plain, axis=1, keepdims=True)
    hidden_grad = plain * p
    up_grad = (hidden_grad * active).astype(BF16)
    gate_grad = (hidden_grad * upper * sigma * (1.0 + gate * (1.0 - sigma))).astype(BF16)
    scaled_hidden = (hidden * p).astype(BF16)
    row_grad = dot(gate_grad, gate_full, ((1,), (1,))) + dot(up_grad, up_full, ((1,), (1,)))
    row_grad = jnp.concatenate(
        [row_grad.astype(BF16), jnp.broadcast_to(prob_grad.astype(BF16), (rows, LANE))], axis=1
    )
    row_grad, gate_grad, up_grad, scaled_hidden = lax.optimization_barrier(
        (row_grad, gate_grad, up_grad, scaled_hidden)
    )
    back = swap(row_grad)
    input_grad = dot(select_rows, back[:, :width], ((0,), (0,))).astype(BF16)
    back_prob = back[:, width].astype(F32).reshape(experts, cap, 1)
    by_expert = jnp.sum(jnp.where(select, back_prob, 0.0), axis=1).T
    prob_out = jnp.sum(jnp.where(picks, by_expert[:, None, :], 0.0), axis=2)

    def share(a, b):
        term = dot(a, b, ((0,), (0,))).astype(BF16)
        return lax.psum_scatter(term, "edp", scatter_dimension=0, tiled=True)[None]

    return (
        input_grad,
        prob_out,
        share(rows_in, gate_grad),
        share(rows_in, up_grad),
        share(scaled_hidden, rows_grad),
    )


def partner(me, bits, d):
    total = 0
    for i in range(bits):
        bit = lax.rem(me // (1 << i), 2)
        total = total + (1 - bit if (d >> i) & 1 else bit) * (1 << i)
    return total


def kernel(quad, cap, hidden, grad, table, wg, wu, wd,
           in_out, prob_out, gw, uw, dw,
           send_in, send_grad, rows_in, rows_grad, send_back, back,
           gate_full, up_full, down_full, active, upper, slope,
           gate_grad, up_grad, scaled, gate_send, up_send, down_send,
           gate_got, up_got, down_got,
           far_table, far_hidden, far_grad, select, relay_in, far_in, relay_prob, far_prob,
           row_send, row_recv, own_sem, w_send, w_recv, w_own, g_send, g_recv, m_send, m_recv):
    me, side = lax.axis_index("ep"), lax.axis_index("edp")
    other = 1 - side
    team, seat = me // quad, lax.rem(me, quad)
    mirror = (1 - team) * quad + seat
    bits = quad.bit_length() - 1
    width, ff = hidden.shape[1], wg.shape[1]
    tok = hidden.shape[0]
    part_rows = quad * cap
    half, down_half = width // 2, ff // 2
    partners = [(d, partner(seat, bits, d)) for d in range(quad - 1, 0, -1)]

    barrier = pltpu.get_barrier_semaphore()
    for d, target in partners:
        pl.semaphore_signal(barrier, inc=1, device_id={"ep": team * quad + target})
    pl.semaphore_signal(barrier, inc=1, device_id={"ep": mirror})
    pl.semaphore_signal(barrier, inc=1, device_id={"edp": other})

    def row_slice(part, owner):
        return pl.ds(pl.multiple_of(part * part_rows + owner * cap, cap), cap)

    def choose(part, entry):
        slot = lax.broadcasted_iota(jnp.int32, (cap, tok), 0).astype(F32)
        for q in range(quad):
            rows = pl.ds(part * part_rows + q * cap, cap)
            mask = entry[q : q + 1, :] == slot
            select[rows, :] = jnp.where(mask, 1.0, 0.0).astype(BF16)
            w = jnp.sum(jnp.where(mask, entry[quad + q : quad + q + 1, :], 0.0), axis=1, keepdims=True)
            send_grad[rows, pl.ds(width, LANE)] = jnp.broadcast_to(w, (cap, LANE)).astype(BF16)

    def dispatch(part, source, sink):
        rows = pl.ds(part * part_rows, part_rows)

        def tile(c, carry):
            cols = pl.ds(pl.multiple_of(c * 512, 512), 512)
            sink[rows, cols] = dot(select[rows, :], source[:, cols], ((1,), (0,))).astype(BF16)
            return carry

        lax.fori_loop(0, width // 512, tile, 0)

    def spread(kind, part, source, sink, low, size):
        cols = pl.ds(low, size)
        copies = []
        for d, target in partners:
            copies.append(pltpu.make_async_remote_copy(
                src_ref=source.at[row_slice(part, target), cols],
                dst_ref=sink.at[row_slice(part, seat), cols],
                send_sem=row_send.at[kind, part, d],
                recv_sem=row_recv.at[kind, part, d],
                device_id={"ep": team * quad + target},
            ))
        for copy in copies:
            copy.start()
        own = pltpu.make_async_copy(
            source.at[row_slice(part, seat), cols], sink.at[row_slice(part, seat), cols],
            own_sem.at[kind, part])
        own.start()
        return copies, own

    def arrive(group):
        copies, own = group
        own.wait()
        for copy in copies:
            copy.wait_recv()

    def cross(i, source, sink):
        copy = pltpu.make_async_remote_copy(
            src_ref=source, dst_ref=sink, send_sem=m_send.at[i], recv_sem=m_recv.at[i],
            device_id={"ep": mirror})
        copy.start()
        return copy

    pl.semaphore_wait(barrier, quad + 1)
    crossed = [cross(0, table.at[1 - team], far_table), cross(1, hidden, far_hidden)]
    choose(0, table[team])
    dispatch(0, hidden, send_in)
    in0 = spread(0, 0, send_in, rows_in, 0, width)

    exchanged = []
    for i, (ref, full) in enumerate(((wg, gate_full), (wu, up_full), (wd, down_full))):
        depth = ref.shape[0]
        place = pl.ds(pl.multiple_of(side * depth, depth), depth)
        copy = pltpu.make_async_remote_copy(
            src_ref=ref, dst_ref=full.at[place], send_sem=w_send.at[i], recv_sem=w_recv.at[i],
            device_id={"edp": other})
        copy.start()
        own = pltpu.make_async_copy(ref, full.at[place], w_own.at[i])
        own.start()
        exchanged.append((copy, own))

    dispatch(0, grad, send_grad)
    crossed[0].wait_recv()
    choose(1, far_table[...])
    crossed[1].wait_send()
    crossed.append(cross(2, grad, far_grad))
    crossed[1].wait_recv()
    dispatch(1, far_hidden, send_in)
    in1 = spread(0, 1, send_in, rows_in, 0, width)
    for copy, own in exchanged:
        own.wait()
        copy.wait_recv()

    def forward(part):
        rows = pl.ds(part * part_rows, part_rows)

        def tile(c, carry):
            cols = pl.ds(pl.multiple_of(c * 256, 256), 256)
            x = rows_in[rows, :]
            gate = dot(x, gate_full[:, cols], ((1,), (0,)))
            up = dot(x, up_full[:, cols], ((1,), (0,)))
            sigma = jax.nn.sigmoid(gate)
            active[rows, cols] = gate * sigma
            upper[rows, cols] = up
            slope[rows, cols] = up * sigma * (1.0 + gate * (1.0 - sigma))
            return carry

        lax.fori_loop(0, ff // 256, tile, 0)

    def backward(part):
        rows = pl.ds(part * part_rows, part_rows)
        p = rows_grad[rows, pl.ds(width, LANE)].astype(F32)[:, :1]

        def tile(c, total):
            cols = pl.ds(pl.multiple_of(c * 256, 256), 256)
            plain = dot(rows_grad[rows, pl.ds(0, width)], down_full[cols, :], ((1,), (1,)))
            act = active[rows, cols]
            hid = act * upper[rows, cols]
            hidden_grad = plain * p
            up_grad[rows, cols] = (hidden_grad * act).astype(BF16)
            gate_grad[rows, cols] = (hidden_grad * slope[rows, cols]).astype(BF16)
            scaled[rows, cols] = (hid * p).astype(BF16)
            return total + jnp.sum(hid * plain, axis=1, keepdims=True)

        total = lax.fori_loop(0, ff // 256, tile, jnp.zeros((part_rows, 1), F32))
        send_back[rows, pl.ds(width, LANE)] = jnp.broadcast_to(total, (part_rows, LANE)).astype(BF16)

    def returns(part, kind, low, size):
        rows = pl.ds(part * part_rows, part_rows)

        def out_tile(c, carry):
            cols = pl.ds(pl.multiple_of(c * 256, 256), 256)
            value = dot(gate_grad[rows, :], gate_full[cols, :], ((1,), (1,)))
            value = value + dot(up_grad[rows, :], up_full[cols, :], ((1,), (1,)))
            send_back[rows, cols] = value.astype(BF16)
            return carry

        lax.fori_loop(low // 256, (low + size) // 256, out_tile, 0)
        tail = LANE if low + size == width else 0
        return spread(kind, part, send_back, back, low, size + tail)

    arrive(in0)
    forward(0)
    crossed[2].wait_send()
    grad0 = spread(1, 0, send_grad, rows_grad, 0, width + LANE)
    crossed[2].wait_recv()
    dispatch(1, far_grad, send_grad)
    grad1 = spread(1, 1, send_grad, rows_grad, 0, width + LANE)
    arrive(in1)
    forward(1)
    arrive(grad0)
    backward(0)
    back0 = returns(0, 2, 0, width)
    arrive(grad1)
    backward(1)
    strip = width // 4
    back1 = [returns(1, 2 + i, i * strip, strip) for i in range(4)]

    def wide(which, sink, factor):
        def tile(c, carry):
            at = pl.ds(pl.multiple_of(which * half + c * 256, 256), 256)
            value = dot(rows_in[:, at], factor[...], ((0,), (0,)))
            sink[pl.ds(pl.multiple_of(c * 256, 256), 256), :] = value.astype(BF16)
            return carry

        lax.fori_loop(0, half // 256, tile, 0)

    def tall(which, sink):
        lhs = pl.ds(pl.multiple_of(which * down_half, LANE), down_half)

        def tile(c, carry):
            cols = pl.ds(pl.multiple_of(c * 512, 512), 512)
            sink[:, cols] = dot(scaled[:, lhs], rows_grad[:, cols], ((0,), (0,))).astype(BF16)
            return carry

        lax.fori_loop(0, width // 512, tile, 0)

    def pass_on(i, source, sink):
        copy = pltpu.make_async_remote_copy(
            src_ref=source, dst_ref=sink, send_sem=g_send.at[i], recv_sem=g_recv.at[i],
            device_id={"edp": other})
        copy.start()
        return copy

    wide(other, gate_send, gate_grad)
    passed = [pass_on(0, gate_send, gate_got)]
    wide(other, up_send, up_grad)
    passed.append(pass_on(1, up_send, up_got))
    tall(other, down_send)
    passed.append(pass_on(2, down_send, down_got))

    def combine(part, sink, low, size, extra=None):
        rows = pl.ds(part * part_rows, part_rows)

        def tile(c, carry):
            cols = pl.ds(pl.multiple_of(c * 512, 512), 512)
            value = dot(select[rows, :], back[rows, cols], ((0,), (0,)))
            if extra is not None:
                value = value + extra[:, cols].astype(F32)
            sink[:, cols] = value.astype(BF16)
            return carry

        lax.fori_loop(low // 512, (low + size) // 512, tile, 0)

    def prob_table(part):
        lines = []
        for q in range(quad):
            rows = pl.ds(part * part_rows + q * cap, cap)
            value = select[rows, :].astype(F32) * back[rows, pl.ds(width, LANE)].astype(F32)
            lines.append(jnp.sum(value, axis=0, keepdims=True))
        return jnp.concatenate(lines + lines, axis=0)

    for i, group in enumerate(back1):
        arrive(group)
        combine(1, relay_in, i * strip, strip)
        cols = pl.ds(i * strip, strip)
        crossed.append(cross(3 + i, relay_in.at[:, cols], far_in.at[:, cols]))
    relay_prob[...] = prob_table(1)
    crossed.append(cross(7, relay_prob, far_prob))
    wide(side, gw, gate_grad)
    wide(side, uw, up_grad)
    tall(side, dw)
    for copy, got, sink in zip(passed, (gate_got, up_got, down_got), (gw, uw, dw)):
        copy.wait_recv()
        steps = sink.shape[0] // 128

        def add(r, carry, got=got, sink=sink):
            at = pl.ds(pl.multiple_of(r * 128, 128), 128)
            sink[at, :] = (sink[at, :].astype(F32) + got[at, :].astype(F32)).astype(BF16)
            return carry

        lax.fori_loop(0, steps, add, 0)

    arrive(back0)
    prob_out[team] = prob_table(0)
    for i in range(4):
        crossed[3 + i].wait_recv()
        combine(0, in_out, i * strip, strip, far_in)
    crossed[7].wait_recv()
    prob_out[1 - team] = far_prob[...]
    for copies, own in (in0, grad0, in1, grad1, back0, *back1):
        for copy in copies:
            copy.wait_send()
    for copy in [crossed[0]] + crossed[3:]:
        copy.wait_send()
    for copy, own in exchanged:
        copy.wait_send()
    for copy in passed:
        copy.wait_send()


def fused(hidden_in, out_grad, routes, probs, w_gate, w_up, w_down):
    tok, top = routes.shape
    width = hidden_in.shape[1]
    ep = lax.axis_size("ep")
    ff = w_gate.shape[2]
    cap = 2 * tok * top // ep
    quad = ep // 2
    rows = ep * cap
    picks, place, weight = routing(routes, probs, ep)
    table = jnp.concatenate(
        [place.T.astype(F32).reshape(2, quad, tok), weight.T.reshape(2, quad, tok)], axis=1
    )
    vmem = pl.BlockSpec(memory_space=pltpu.VMEM)
    hbm = pl.BlockSpec(memory_space=pl.ANY)

    def buf(*shape, dtype=BF16):
        return pltpu.VMEM(shape, dtype)

    wide, down = (width // 2, ff), (ff // 2, width)
    dma = pltpu.SemaphoreType.DMA
    input_grad, back_prob, gw, uw, dw = pl.pallas_call(
        functools.partial(kernel, quad, cap),
        out_shape=(
            jax.ShapeDtypeStruct((tok, width), BF16),
            jax.ShapeDtypeStruct((2, ep, tok), F32),
            jax.ShapeDtypeStruct(wide, BF16),
            jax.ShapeDtypeStruct(wide, BF16),
            jax.ShapeDtypeStruct(down, BF16),
        ),
        in_specs=[vmem] * 3 + [hbm] * 3,
        out_specs=(vmem,) * 5,
        scratch_shapes=[
            buf(rows, width), buf(rows, width + LANE), buf(rows, width), buf(rows, width + LANE),
            buf(rows, width + LANE), buf(rows, width + LANE),
            buf(width, ff), buf(width, ff), buf(ff, width),
            buf(rows, ff, dtype=F32), buf(rows, ff, dtype=F32), buf(rows, ff, dtype=F32),
            buf(rows, ff), buf(rows, ff), buf(rows, ff),
            buf(*wide), buf(*wide), buf(*down), buf(*wide), buf(*wide), buf(*down),
            buf(ep, tok, dtype=F32), buf(tok, width), buf(tok, width), buf(rows, tok),
            buf(tok, width), buf(tok, width), buf(ep, tok, dtype=F32), buf(ep, tok, dtype=F32),
            dma((6, 2, quad)), dma((6, 2, quad)), dma((6, 2)),
            dma((3,)), dma((3,)), dma((3,)), dma((3,)), dma((3,)), dma((8,)), dma((8,)),
        ],
        compiler_params=pltpu.CompilerParams(
            collective_id=0, has_side_effects=True, vmem_limit_bytes=60 << 20
        ),
        cost_estimate=pl.CostEstimate(
            flops=16 * rows * width * ff, bytes_accessed=24 * rows * width, transcendentals=rows * ff
        ),
    )(hidden_in, out_grad, table, w_gate[0], w_up[0], w_down[0])
    by_expert = back_prob[:, :quad].reshape(ep, tok).T
    prob_grad = jnp.sum(jnp.where(picks, by_expert[:, None, :], 0.0), axis=2)
    return input_grad, prob_grad, gw[None], uw[None], dw[None]


def local(*arrays):
    tok, top = arrays[2].shape
    width, ff = arrays[4].shape[1] * 2, arrays[4].shape[2]
    ep = lax.axis_size("ep")
    whole_tiles = tok % 128 == 0 and width % 2048 == 0 and ff % 256 == 0
    one_each = arrays[4].shape[0] == 1 and lax.axis_size("edp") == 2
    if one_each and whole_tiles and ep == 8 and tok == LANE and 2 * tok * top // ep % 32 == 0:
        return fused(*arrays)
    return general(*arrays)


def solution(mesh):
    tokens = P(("groups", "ep", "edp"), None)
    weights = P("ep", "edp", None)
    grads = P(("groups", "ep"), "edp", None)
    return jax.shard_map(
        local,
        mesh=mesh,
        in_specs=(tokens,) * 4 + (weights,) * 3,
        out_specs=(tokens, tokens, grads, grads, grads),
        check_vma=False,
    )
```

```python
import functools

import jax
import jax.numpy as jnp
from jax import lax
from jax.experimental import pallas as pl
from jax.experimental.pallas import tpu as pltpu
from jax.sharding import PartitionSpec as P

F32 = jnp.float32
BF16 = jnp.bfloat16
LANE = 128


def dot(a, b, dims):
    return lax.dot_general(a, b, (dims, ((), ())), preferred_element_type=F32)


def routing(routes, probs, experts):
    tok, top = routes.shape
    picks = routes[:, :, None] == jnp.arange(experts, dtype=jnp.int32)[None, None, :]
    chosen = jnp.any(picks, axis=1)
    weight = jnp.sum(jnp.where(picks, probs[:, :, None], 0.0), axis=1)
    order = jnp.arange(tok, dtype=jnp.int32)
    earlier = (order[:, None] > order[None, :]).astype(BF16)
    place = dot(earlier, chosen.astype(BF16), ((1,), (0,))).astype(jnp.int32)
    place = jnp.where(chosen, place, -1)
    return picks, place, weight


def general(hidden_in, out_grad, routes, probs, w_gate, w_up, w_down):
    tok, top = routes.shape
    width = hidden_in.shape[1]
    ep = lax.axis_size("ep")
    experts = ep * w_gate.shape[0]
    cap = max(8, 2 * tok * top // experts)
    rows = experts * cap
    picks, place, weight = routing(routes, probs, experts)
    slot = jnp.arange(cap, dtype=jnp.int32)
    select = place.T[:, None, :] == slot[None, :, None]
    select_rows = select.reshape(rows, tok).astype(BF16)
    row_weight = jnp.sum(jnp.where(select, weight.T[:, None, :], 0.0), axis=2).reshape(rows, 1)
    send_in = dot(select_rows, hidden_in, ((1,), (0,))).astype(BF16)
    send_grad = dot(select_rows, out_grad, ((1,), (0,))).astype(BF16)
    send_grad = jnp.concatenate(
        [send_grad, jnp.broadcast_to(row_weight.astype(BF16), (rows, LANE))], axis=1
    )

    def swap(value):
        return lax.all_to_all(
            value.reshape(experts, cap, -1), "ep", split_axis=0, concat_axis=0, tiled=True
        ).reshape(rows, -1)

    gate_full, up_full, down_full = (
        lax.all_gather(w[0], "edp", axis=0, tiled=True) for w in (w_gate, w_up, w_down)
    )
    rows_in = swap(send_in)
    got = swap(send_grad)
    rows_grad = got[:, :width]
    p = got[:, width : width + 1].astype(F32)
    gate = dot(rows_in, gate_full, ((1,), (0,)))
    upper = dot(rows_in, up_full, ((1,), (0,)))
    sigma = jax.nn.sigmoid(gate)
    active = gate * sigma
    hidden = active * upper
    plain = dot(rows_grad, down_full, ((1,), (1,)))
    prob_grad = jnp.sum(hidden * plain, axis=1, keepdims=True)
    hidden_grad = plain * p
    up_grad = (hidden_grad * active).astype(BF16)
    gate_grad = (hidden_grad * upper * sigma * (1.0 + gate * (1.0 - sigma))).astype(BF16)
    scaled_hidden = (hidden * p).astype(BF16)
    row_grad = dot(gate_grad, gate_full, ((1,), (1,))) + dot(up_grad, up_full, ((1,), (1,)))
    row_grad = jnp.concatenate(
        [row_grad.astype(BF16), jnp.broadcast_to(prob_grad.astype(BF16), (rows, LANE))], axis=1
    )
    row_grad, gate_grad, up_grad, scaled_hidden = lax.optimization_barrier(
        (row_grad, gate_grad, up_grad, scaled_hidden)
    )
    back = swap(row_grad)
    input_grad = dot(select_rows, back[:, :width], ((0,), (0,))).astype(BF16)
    back_prob = back[:, width].astype(F32).reshape(experts, cap, 1)
    by_expert = jnp.sum(jnp.where(select, back_prob, 0.0), axis=1).T
    prob_out = jnp.sum(jnp.where(picks, by_expert[:, None, :], 0.0), axis=2)

    def share(a, b):
        term = dot(a, b, ((0,), (0,))).astype(BF16)
        return lax.psum_scatter(term, "edp", scatter_dimension=0, tiled=True)[None]

    return (
        input_grad,
        prob_out,
        share(rows_in, gate_grad),
        share(rows_in, up_grad),
        share(scaled_hidden, rows_grad),
    )


def partner(me, bits, d):
    total = 0
    for i in range(bits):
        bit = lax.rem(me // (1 << i), 2)
        total = total + (1 - bit if (d >> i) & 1 else bit) * (1 << i)
    return total


def kernel(quad, cap, hidden, grad, table, wg, wu, wd,
           in_out, prob_out, gw, uw, dw,
           send_in, send_grad, rows_in, rows_grad, send_back, back,
           gate_full, up_full, down_full, active, upper, slope,
           gate_grad, up_grad, scaled, gate_send, up_send, down_send,
           gate_got, up_got, down_got,
           far_table, far_hidden, far_grad, select, relay_in, far_in, relay_prob, far_prob,
           row_send, row_recv, own_sem, w_send, w_recv, w_own, g_send, g_recv, m_send, m_recv):
    me, side = lax.axis_index("ep"), lax.axis_index("edp")
    other = 1 - side
    team, seat = me // quad, lax.rem(me, quad)
    mirror = (1 - team) * quad + seat
    bits = quad.bit_length() - 1
    width, ff = hidden.shape[1], wg.shape[1]
    tok = hidden.shape[0]
    part_rows = quad * cap
    half, down_half = width // 2, ff // 2
    partners = [(d, partner(seat, bits, d)) for d in range(quad - 1, 0, -1)]

    barrier = pltpu.get_barrier_semaphore()
    for d, target in partners:
        pl.semaphore_signal(barrier, inc=1, device_id={"ep": team * quad + target})
    pl.semaphore_signal(barrier, inc=1, device_id={"ep": mirror})
    pl.semaphore_signal(barrier, inc=1, device_id={"edp": other})

    def row_slice(part, owner):
        return pl.ds(pl.multiple_of(part * part_rows + owner * cap, cap), cap)

    def choose(part, entry):
        slot = lax.broadcasted_iota(jnp.int32, (cap, tok), 0).astype(F32)
        for q in range(quad):
            rows = pl.ds(part * part_rows + q * cap, cap)
            mask = entry[q : q + 1, :] == slot
            select[rows, :] = jnp.where(mask, 1.0, 0.0).astype(BF16)
            w = jnp.sum(jnp.where(mask, entry[quad + q : quad + q + 1, :], 0.0), axis=1, keepdims=True)
            send_grad[rows, pl.ds(width, LANE)] = jnp.broadcast_to(w, (cap, LANE)).astype(BF16)

    def dispatch(part, source, sink):
        rows = pl.ds(part * part_rows, part_rows)

        def tile(c, carry):
            cols = pl.ds(pl.multiple_of(c * 512, 512), 512)
            sink[rows, cols] = dot(select[rows, :], source[:, cols], ((1,), (0,))).astype(BF16)
            return carry

        lax.fori_loop(0, width // 512, tile, 0)

    def spread(kind, part, source, sink, low, size):
        cols = pl.ds(low, size)
        copies = []
        for d, target in partners:
            copies.append(pltpu.make_async_remote_copy(
                src_ref=source.at[row_slice(part, target), cols],
                dst_ref=sink.at[row_slice(part, seat), cols],
                send_sem=row_send.at[kind, part, d],
                recv_sem=row_recv.at[kind, part, d],
                device_id={"ep": team * quad + target},
            ))
        for copy in copies:
            copy.start()
        own = pltpu.make_async_copy(
            source.at[row_slice(part, seat), cols], sink.at[row_slice(part, seat), cols],
            own_sem.at[kind, part])
        own.start()
        return copies, own

    def arrive(group):
        copies, own = group
        own.wait()
        for copy in copies:
            copy.wait_recv()

    def cross(i, source, sink):
        copy = pltpu.make_async_remote_copy(
            src_ref=source, dst_ref=sink, send_sem=m_send.at[i], recv_sem=m_recv.at[i],
            device_id={"ep": mirror})
        copy.start()
        return copy

    pl.semaphore_wait(barrier, quad + 1)
    crossed = [cross(0, table.at[1 - team], far_table), cross(1, hidden, far_hidden)]
    choose(0, table[team])
    dispatch(0, hidden, send_in)
    in0 = spread(0, 0, send_in, rows_in, 0, width)
    crossed.append(cross(2, grad, far_grad))
    dispatch(0, grad, send_grad)
    grad0 = spread(1, 0, send_grad, rows_grad, 0, width + LANE)

    exchanged = []
    for i, (ref, full) in enumerate(((wg, gate_full), (wu, up_full), (wd, down_full))):
        depth = ref.shape[0]
        place = pl.ds(pl.multiple_of(side * depth, depth), depth)
        copy = pltpu.make_async_remote_copy(
            src_ref=ref, dst_ref=full.at[place], send_sem=w_send.at[i], recv_sem=w_recv.at[i],
            device_id={"edp": other})
        copy.start()
        own = pltpu.make_async_copy(ref, full.at[place], w_own.at[i])
        own.start()
        exchanged.append((copy, own))

    crossed[0].wait_recv()
    choose(1, far_table[...])
    crossed[1].wait_recv()
    dispatch(1, far_hidden, send_in)
    in1 = spread(0, 1, send_in, rows_in, 0, width)
    for copy, own in exchanged:
        own.wait()
        copy.wait_recv()

    def forward(part):
        rows = pl.ds(part * part_rows, part_rows)

        def tile(c, carry):
            cols = pl.ds(pl.multiple_of(c * 256, 256), 256)
            x = rows_in[rows, :]
            gate = dot(x, gate_full[:, cols], ((1,), (0,)))
            up = dot(x, up_full[:, cols], ((1,), (0,)))
            sigma = jax.nn.sigmoid(gate)
            active[rows, cols] = gate * sigma
            upper[rows, cols] = up
            slope[rows, cols] = up * sigma * (1.0 + gate * (1.0 - sigma))
            return carry

        lax.fori_loop(0, ff // 256, tile, 0)

    def backward(part):
        rows = pl.ds(part * part_rows, part_rows)
        p = rows_grad[rows, pl.ds(width, LANE)].astype(F32)[:, :1]

        def tile(c, total):
            cols = pl.ds(pl.multiple_of(c * 256, 256), 256)
            plain = dot(rows_grad[rows, pl.ds(0, width)], down_full[cols, :], ((1,), (1,)))
            act = active[rows, cols]
            hid = act * upper[rows, cols]
            hidden_grad = plain * p
            up_grad[rows, cols] = (hidden_grad * act).astype(BF16)
            gate_grad[rows, cols] = (hidden_grad * slope[rows, cols]).astype(BF16)
            scaled[rows, cols] = (hid * p).astype(BF16)
            return total + jnp.sum(hid * plain, axis=1, keepdims=True)

        total = lax.fori_loop(0, ff // 256, tile, jnp.zeros((part_rows, 1), F32))
        send_back[rows, pl.ds(width, LANE)] = jnp.broadcast_to(total, (part_rows, LANE)).astype(BF16)

    def returns(part, kind, low, size):
        rows = pl.ds(part * part_rows, part_rows)

        def out_tile(c, carry):
            cols = pl.ds(pl.multiple_of(c * 256, 256), 256)
            value = dot(gate_grad[rows, :], gate_full[cols, :], ((1,), (1,)))
            value = value + dot(up_grad[rows, :], up_full[cols, :], ((1,), (1,)))
            send_back[rows, cols] = value.astype(BF16)
            return carry

        lax.fori_loop(low // 256, (low + size) // 256, out_tile, 0)
        tail = LANE if low + size == width else 0
        return spread(kind, part, send_back, back, low, size + tail)

    arrive(in0)
    forward(0)
    crossed[2].wait_recv()
    dispatch(1, far_grad, send_grad)
    grad1 = spread(1, 1, send_grad, rows_grad, 0, width + LANE)
    arrive(grad0)
    backward(0)
    back0 = returns(0, 2, 0, width)
    arrive(in1)
    forward(1)
    arrive(grad1)
    backward(1)
    strip = width // 4
    back1 = [returns(1, 2 + i, i * strip, strip) for i in range(4)]

    def wide(which, sink, factor):
        def tile(c, carry):
            at = pl.ds(pl.multiple_of(which * half + c * 256, 256), 256)
            value = dot(rows_in[:, at], factor[...], ((0,), (0,)))
            sink[pl.ds(pl.multiple_of(c * 256, 256), 256), :] = value.astype(BF16)
            return carry

        lax.fori_loop(0, half // 256, tile, 0)

    def tall(which, sink):
        lhs = pl.ds(pl.multiple_of(which * down_half, LANE), down_half)

        def tile(c, carry):
            cols = pl.ds(pl.multiple_of(c * 512, 512), 512)
            sink[:, cols] = dot(scaled[:, lhs], rows_grad[:, cols], ((0,), (0,))).astype(BF16)
            return carry

        lax.fori_loop(0, width // 512, tile, 0)

    def pass_on(i, source, sink):
        copy = pltpu.make_async_remote_copy(
            src_ref=source, dst_ref=sink, send_sem=g_send.at[i], recv_sem=g_recv.at[i],
            device_id={"edp": other})
        copy.start()
        return copy

    wide(other, gate_send, gate_grad)
    passed = [pass_on(0, gate_send, gate_got)]
    wide(other, up_send, up_grad)
    passed.append(pass_on(1, up_send, up_got))
    tall(other, down_send)
    passed.append(pass_on(2, down_send, down_got))

    def combine(part, sink, low, size, extra=None):
        rows = pl.ds(part * part_rows, part_rows)

        def tile(c, carry):
            cols = pl.ds(pl.multiple_of(c * 512, 512), 512)
            value = dot(select[rows, :], back[rows, cols], ((0,), (0,)))
            if extra is not None:
                value = value + extra[:, cols].astype(F32)
            sink[:, cols] = value.astype(BF16)
            return carry

        lax.fori_loop(low // 512, (low + size) // 512, tile, 0)

    def prob_table(part):
        lines = []
        for q in range(quad):
            rows = pl.ds(part * part_rows + q * cap, cap)
            value = select[rows, :].astype(F32) * back[rows, pl.ds(width, LANE)].astype(F32)
            lines.append(jnp.sum(value, axis=0, keepdims=True))
        return jnp.concatenate(lines + lines, axis=0)

    for i, group in enumerate(back1):
        arrive(group)
        combine(1, relay_in, i * strip, strip)
        cols = pl.ds(i * strip, strip)
        crossed.append(cross(3 + i, relay_in.at[:, cols], far_in.at[:, cols]))
    relay_prob[...] = prob_table(1)
    crossed.append(cross(7, relay_prob, far_prob))
    wide(side, gw, gate_grad)
    wide(side, uw, up_grad)
    tall(side, dw)
    for copy, got, sink in zip(passed, (gate_got, up_got, down_got), (gw, uw, dw)):
        copy.wait_recv()
        steps = sink.shape[0] // 128

        def add(r, carry, got=got, sink=sink):
            at = pl.ds(pl.multiple_of(r * 128, 128), 128)
            sink[at, :] = (sink[at, :].astype(F32) + got[at, :].astype(F32)).astype(BF16)
            return carry

        lax.fori_loop(0, steps, add, 0)

    arrive(back0)
    prob_out[team] = prob_table(0)
    for i in range(4):
        crossed[3 + i].wait_recv()
        combine(0, in_out, i * strip, strip, far_in)
    crossed[7].wait_recv()
    prob_out[1 - team] = far_prob[...]
    for copies, own in (in0, grad0, in1, grad1, back0, *back1):
        for copy in copies:
            copy.wait_send()
    for copy in crossed:
        copy.wait_send()
    for copy, own in exchanged:
        copy.wait_send()
    for copy in passed:
        copy.wait_send()


def fused(hidden_in, out_grad, routes, probs, w_gate, w_up, w_down):
    tok, top = routes.shape
    width = hidden_in.shape[1]
    ep = lax.axis_size("ep")
    ff = w_gate.shape[2]
    cap = 2 * tok * top // ep
    quad = ep // 2
    rows = ep * cap
    picks, place, weight = routing(routes, probs, ep)
    table = jnp.concatenate(
        [place.T.astype(F32).reshape(2, quad, tok), weight.T.reshape(2, quad, tok)], axis=1
    )
    vmem = pl.BlockSpec(memory_space=pltpu.VMEM)
    hbm = pl.BlockSpec(memory_space=pl.ANY)

    def buf(*shape, dtype=BF16):
        return pltpu.VMEM(shape, dtype)

    wide, down = (width // 2, ff), (ff // 2, width)
    dma = pltpu.SemaphoreType.DMA
    input_grad, back_prob, gw, uw, dw = pl.pallas_call(
        functools.partial(kernel, quad, cap),
        out_shape=(
            jax.ShapeDtypeStruct((tok, width), BF16),
            jax.ShapeDtypeStruct((2, ep, tok), F32),
            jax.ShapeDtypeStruct(wide, BF16),
            jax.ShapeDtypeStruct(wide, BF16),
            jax.ShapeDtypeStruct(down, BF16),
        ),
        in_specs=[vmem] * 3 + [hbm] * 3,
        out_specs=(vmem,) * 5,
        scratch_shapes=[
            buf(rows, width), buf(rows, width + LANE), buf(rows, width), buf(rows, width + LANE),
            buf(rows, width + LANE), buf(rows, width + LANE),
            buf(width, ff), buf(width, ff), buf(ff, width),
            buf(rows, ff, dtype=F32), buf(rows, ff, dtype=F32), buf(rows, ff, dtype=F32),
            buf(rows, ff), buf(rows, ff), buf(rows, ff),
            buf(*wide), buf(*wide), buf(*down), buf(*wide), buf(*wide), buf(*down),
            buf(ep, tok, dtype=F32), buf(tok, width), buf(tok, width), buf(rows, tok),
            buf(tok, width), buf(tok, width), buf(ep, tok, dtype=F32), buf(ep, tok, dtype=F32),
            dma((6, 2, quad)), dma((6, 2, quad)), dma((6, 2)),
            dma((3,)), dma((3,)), dma((3,)), dma((3,)), dma((3,)), dma((8,)), dma((8,)),
        ],
        compiler_params=pltpu.CompilerParams(
            collective_id=0, has_side_effects=True, vmem_limit_bytes=60 << 20
        ),
        cost_estimate=pl.CostEstimate(
            flops=16 * rows * width * ff, bytes_accessed=24 * rows * width, transcendentals=rows * ff
        ),
    )(hidden_in, out_grad, table, w_gate[0], w_up[0], w_down[0])
    by_expert = back_prob[:, :quad].reshape(ep, tok).T
    prob_grad = jnp.sum(jnp.where(picks, by_expert[:, None, :], 0.0), axis=2)
    return input_grad, prob_grad, gw[None], uw[None], dw[None]


def local(*arrays):
    tok, top = arrays[2].shape
    width, ff = arrays[4].shape[1] * 2, arrays[4].shape[2]
    ep = lax.axis_size("ep")
    whole_tiles = tok % 128 == 0 and width % 2048 == 0 and ff % 256 == 0
    one_each = arrays[4].shape[0] == 1 and lax.axis_size("edp") == 2
    if one_each and whole_tiles and ep == 8 and tok == LANE and 2 * tok * top // ep % 32 == 0:
        return fused(*arrays)
    return general(*arrays)


def solution(mesh):
    tokens = P(("groups", "ep", "edp"), None)
    weights = P("ep", "edp", None)
    grads = P(("groups", "ep"), "edp", None)
    return jax.shard_map(
        local,
        mesh=mesh,
        in_specs=(tokens,) * 4 + (weights,) * 3,
        out_specs=(tokens, tokens, grads, grads, grads),
        check_vma=False,
    )
```

```python
import functools

import jax
import jax.numpy as jnp
from jax import lax
from jax.experimental import pallas as pl
from jax.experimental.pallas import tpu as pltpu
from jax.sharding import PartitionSpec as P

F32 = jnp.float32
BF16 = jnp.bfloat16
LANE = 128


def dot(a, b, dims):
    return lax.dot_general(a, b, (dims, ((), ())), preferred_element_type=F32)


def routing(routes, probs, experts):
    tok, top = routes.shape
    picks = routes[:, :, None] == jnp.arange(experts, dtype=jnp.int32)[None, None, :]
    chosen = jnp.any(picks, axis=1)
    weight = jnp.sum(jnp.where(picks, probs[:, :, None], 0.0), axis=1)
    order = jnp.arange(tok, dtype=jnp.int32)
    earlier = (order[:, None] > order[None, :]).astype(BF16)
    place = dot(earlier, chosen.astype(BF16), ((1,), (0,))).astype(jnp.int32)
    place = jnp.where(chosen, place, -1)
    return picks, place, weight


def general(hidden_in, out_grad, routes, probs, w_gate, w_up, w_down):
    tok, top = routes.shape
    width = hidden_in.shape[1]
    ep = lax.axis_size("ep")
    experts = ep * w_gate.shape[0]
    cap = max(8, 2 * tok * top // experts)
    rows = experts * cap
    picks, place, weight = routing(routes, probs, experts)
    slot = jnp.arange(cap, dtype=jnp.int32)
    select = place.T[:, None, :] == slot[None, :, None]
    select_rows = select.reshape(rows, tok).astype(BF16)
    row_weight = jnp.sum(jnp.where(select, weight.T[:, None, :], 0.0), axis=2).reshape(rows, 1)
    send_in = dot(select_rows, hidden_in, ((1,), (0,))).astype(BF16)
    send_grad = dot(select_rows, out_grad, ((1,), (0,))).astype(BF16)
    send_grad = jnp.concatenate(
        [send_grad, jnp.broadcast_to(row_weight.astype(BF16), (rows, LANE))], axis=1
    )

    def swap(value):
        return lax.all_to_all(
            value.reshape(experts, cap, -1), "ep", split_axis=0, concat_axis=0, tiled=True
        ).reshape(rows, -1)

    gate_full, up_full, down_full = (
        lax.all_gather(w[0], "edp", axis=0, tiled=True) for w in (w_gate, w_up, w_down)
    )
    rows_in = swap(send_in)
    got = swap(send_grad)
    rows_grad = got[:, :width]
    p = got[:, width : width + 1].astype(F32)
    gate = dot(rows_in, gate_full, ((1,), (0,)))
    upper = dot(rows_in, up_full, ((1,), (0,)))
    sigma = jax.nn.sigmoid(gate)
    active = gate * sigma
    hidden = active * upper
    plain = dot(rows_grad, down_full, ((1,), (1,)))
    prob_grad = jnp.sum(hidden * plain, axis=1, keepdims=True)
    hidden_grad = plain * p
    up_grad = (hidden_grad * active).astype(BF16)
    gate_grad = (hidden_grad * upper * sigma * (1.0 + gate * (1.0 - sigma))).astype(BF16)
    scaled_hidden = (hidden * p).astype(BF16)
    row_grad = dot(gate_grad, gate_full, ((1,), (1,))) + dot(up_grad, up_full, ((1,), (1,)))
    row_grad = jnp.concatenate(
        [row_grad.astype(BF16), jnp.broadcast_to(prob_grad.astype(BF16), (rows, LANE))], axis=1
    )
    row_grad, gate_grad, up_grad, scaled_hidden = lax.optimization_barrier(
        (row_grad, gate_grad, up_grad, scaled_hidden)
    )
    back = swap(row_grad)
    input_grad = dot(select_rows, back[:, :width], ((0,), (0,))).astype(BF16)
    back_prob = back[:, width].astype(F32).reshape(experts, cap, 1)
    by_expert = jnp.sum(jnp.where(select, back_prob, 0.0), axis=1).T
    prob_out = jnp.sum(jnp.where(picks, by_expert[:, None, :], 0.0), axis=2)

    def share(a, b):
        term = dot(a, b, ((0,), (0,))).astype(BF16)
        return lax.psum_scatter(term, "edp", scatter_dimension=0, tiled=True)[None]

    return (
        input_grad,
        prob_out,
        share(rows_in, gate_grad),
        share(rows_in, up_grad),
        share(scaled_hidden, rows_grad),
    )


def partner(me, bits, d):
    total = 0
    for i in range(bits):
        bit = lax.rem(me // (1 << i), 2)
        total = total + (1 - bit if (d >> i) & 1 else bit) * (1 << i)
    return total


def kernel(quad, cap, hidden, grad, table, wg, wu, wd,
           in_out, prob_out, gw, uw, dw,
           send_in, send_grad, rows_in, rows_grad, send_back, back,
           gate_full, up_full, down_full, active, upper, slope,
           gate_grad, up_grad, scaled, gate_send, up_send, down_send,
           gate_got, up_got, down_got,
           far_table, far_hidden, far_grad, select, relay_in, far_in, relay_prob, far_prob,
           row_send, row_recv, own_sem, w_send, w_recv, w_own, g_send, g_recv, m_send, m_recv):
    me, side = lax.axis_index("ep"), lax.axis_index("edp")
    other = 1 - side
    team, seat = me // quad, lax.rem(me, quad)
    mirror = (1 - team) * quad + seat
    bits = quad.bit_length() - 1
    width, ff = hidden.shape[1], wg.shape[1]
    tok = hidden.shape[0]
    part_rows = quad * cap
    half, down_half = width // 2, ff // 2
    partners = [(d, partner(seat, bits, d)) for d in range(quad - 1, 0, -1)]

    barrier = pltpu.get_barrier_semaphore()
    for d, target in partners:
        pl.semaphore_signal(barrier, inc=1, device_id={"ep": team * quad + target})
    pl.semaphore_signal(barrier, inc=1, device_id={"ep": mirror})
    pl.semaphore_signal(barrier, inc=1, device_id={"edp": other})

    def row_slice(part, owner):
        return pl.ds(pl.multiple_of(part * part_rows + owner * cap, cap), cap)

    def choose(part, entry):
        slot = lax.broadcasted_iota(jnp.int32, (cap, tok), 0).astype(F32)
        for q in range(quad):
            rows = pl.ds(part * part_rows + q * cap, cap)
            mask = entry[q : q + 1, :] == slot
            select[rows, :] = jnp.where(mask, 1.0, 0.0).astype(BF16)
            w = jnp.sum(jnp.where(mask, entry[quad + q : quad + q + 1, :], 0.0), axis=1, keepdims=True)
            send_grad[rows, pl.ds(width, LANE)] = jnp.broadcast_to(w, (cap, LANE)).astype(BF16)

    def dispatch(part, source, sink):
        rows = pl.ds(part * part_rows, part_rows)

        def tile(c, carry):
            cols = pl.ds(pl.multiple_of(c * 512, 512), 512)
            sink[rows, cols] = dot(select[rows, :], source[:, cols], ((1,), (0,))).astype(BF16)
            return carry

        lax.fori_loop(0, width // 512, tile, 0)

    def spread(kind, part, source, sink, low, size):
        cols = pl.ds(low, size)
        copies = []
        for d, target in partners:
            copies.append(pltpu.make_async_remote_copy(
                src_ref=source.at[row_slice(part, target), cols],
                dst_ref=sink.at[row_slice(part, seat), cols],
                send_sem=row_send.at[kind, part, d],
                recv_sem=row_recv.at[kind, part, d],
                device_id={"ep": team * quad + target},
            ))
        for copy in copies:
            copy.start()
        own = pltpu.make_async_copy(
            source.at[row_slice(part, seat), cols], sink.at[row_slice(part, seat), cols],
            own_sem.at[kind, part])
        own.start()
        return copies, own

    def arrive(group):
        copies, own = group
        own.wait()
        for copy in copies:
            copy.wait_recv()

    def cross(i, source, sink):
        copy = pltpu.make_async_remote_copy(
            src_ref=source, dst_ref=sink, send_sem=m_send.at[i], recv_sem=m_recv.at[i],
            device_id={"ep": mirror})
        copy.start()
        return copy

    pl.semaphore_wait(barrier, quad + 1)
    crossed = [cross(0, table.at[1 - team], far_table), cross(1, hidden, far_hidden)]
    choose(0, table[team])
    dispatch(0, hidden, send_in)
    in0 = spread(0, 0, send_in, rows_in, 0, width)
    crossed.append(cross(2, grad, far_grad))
    dispatch(0, grad, send_grad)
    grad0 = spread(1, 0, send_grad, rows_grad, 0, width + LANE)

    exchanged = []
    for i, (ref, full) in enumerate(((wg, gate_full), (wu, up_full), (wd, down_full))):
        depth = ref.shape[0]
        place = pl.ds(pl.multiple_of(side * depth, depth), depth)
        copy = pltpu.make_async_remote_copy(
            src_ref=ref, dst_ref=full.at[place], send_sem=w_send.at[i], recv_sem=w_recv.at[i],
            device_id={"edp": other})
        copy.start()
        own = pltpu.make_async_copy(ref, full.at[place], w_own.at[i])
        own.start()
        exchanged.append((copy, own))

    crossed[0].wait_recv()
    choose(1, far_table[...])
    crossed[1].wait_recv()
    dispatch(1, far_hidden, send_in)
    in1 = spread(0, 1, send_in, rows_in, 0, width)
    for copy, own in exchanged:
        own.wait()
        copy.wait_recv()

    def forward(part):
        rows = pl.ds(part * part_rows, part_rows)

        def tile(c, carry):
            cols = pl.ds(pl.multiple_of(c * 256, 256), 256)
            x = rows_in[rows, :]
            gate = dot(x, gate_full[:, cols], ((1,), (0,)))
            up = dot(x, up_full[:, cols], ((1,), (0,)))
            sigma = jax.nn.sigmoid(gate)
            active[rows, cols] = gate * sigma
            upper[rows, cols] = up
            slope[rows, cols] = up * sigma * (1.0 + gate * (1.0 - sigma))
            return carry

        lax.fori_loop(0, ff // 256, tile, 0)

    def backward(part):
        rows = pl.ds(part * part_rows, part_rows)
        p = rows_grad[rows, pl.ds(width, LANE)].astype(F32)[:, :1]

        def tile(c, total):
            cols = pl.ds(pl.multiple_of(c * 256, 256), 256)
            plain = dot(rows_grad[rows, pl.ds(0, width)], down_full[cols, :], ((1,), (1,)))
            act = active[rows, cols]
            hid = act * upper[rows, cols]
            hidden_grad = plain * p
            up_grad[rows, cols] = (hidden_grad * act).astype(BF16)
            gate_grad[rows, cols] = (hidden_grad * slope[rows, cols]).astype(BF16)
            scaled[rows, cols] = (hid * p).astype(BF16)
            return total + jnp.sum(hid * plain, axis=1, keepdims=True)

        total = lax.fori_loop(0, ff // 256, tile, jnp.zeros((part_rows, 1), F32))
        send_back[rows, pl.ds(width, LANE)] = jnp.broadcast_to(total, (part_rows, LANE)).astype(BF16)

    def returns(part, kind, low, size):
        rows = pl.ds(part * part_rows, part_rows)

        def out_tile(c, carry):
            cols = pl.ds(pl.multiple_of(c * 256, 256), 256)
            value = dot(gate_grad[rows, :], gate_full[cols, :], ((1,), (1,)))
            value = value + dot(up_grad[rows, :], up_full[cols, :], ((1,), (1,)))
            send_back[rows, cols] = value.astype(BF16)
            return carry

        lax.fori_loop(low // 256, (low + size) // 256, out_tile, 0)
        tail = LANE if low + size == width else 0
        return spread(kind, part, send_back, back, low, size + tail)

    arrive(in0)
    forward(0)
    crossed[2].wait_recv()
    dispatch(1, far_grad, send_grad)
    grad1 = spread(1, 1, send_grad, rows_grad, 0, width + LANE)
    arrive(grad0)
    backward(0)
    back0 = returns(0, 2, 0, width)
    arrive(in1)
    forward(1)
    arrive(grad1)
    backward(1)
    strip = width // 4
    back1 = [returns(1, 2 + i, i * strip, strip) for i in range(4)]

    def wide(which, sink, factor):
        def tile(c, carry):
            at = pl.ds(pl.multiple_of(which * half + c * 256, 256), 256)
            value = dot(rows_in[:, at], factor[...], ((0,), (0,)))
            sink[pl.ds(pl.multiple_of(c * 256, 256), 256), :] = value.astype(BF16)
            return carry

        lax.fori_loop(0, half // 256, tile, 0)

    def tall(which, sink):
        lhs = pl.ds(pl.multiple_of(which * down_half, LANE), down_half)

        def tile(c, carry):
            cols = pl.ds(pl.multiple_of(c * 512, 512), 512)
            sink[:, cols] = dot(scaled[:, lhs], rows_grad[:, cols], ((0,), (0,))).astype(BF16)
            return carry

        lax.fori_loop(0, width // 512, tile, 0)

    def pass_on(i, source, sink):
        copy = pltpu.make_async_remote_copy(
            src_ref=source, dst_ref=sink, send_sem=g_send.at[i], recv_sem=g_recv.at[i],
            device_id={"edp": other})
        copy.start()
        return copy

    passed = []
    def combine(part, sink, low, size, extra=None):
        rows = pl.ds(part * part_rows, part_rows)

        def tile(c, carry):
            cols = pl.ds(pl.multiple_of(c * 512, 512), 512)
            value = dot(select[rows, :], back[rows, cols], ((0,), (0,)))
            if extra is not None:
                value = value + extra[:, cols].astype(F32)
            sink[:, cols] = value.astype(BF16)
            return carry

        lax.fori_loop(low // 512, (low + size) // 512, tile, 0)

    def prob_table(part):
        lines = []
        for q in range(quad):
            rows = pl.ds(part * part_rows + q * cap, cap)
            value = select[rows, :].astype(F32) * back[rows, pl.ds(width, LANE)].astype(F32)
            lines.append(jnp.sum(value, axis=0, keepdims=True))
        return jnp.concatenate(lines + lines, axis=0)

    for i, group in enumerate(back1):
        arrive(group)
        combine(1, relay_in, i * strip, strip)
        cols = pl.ds(i * strip, strip)
        crossed.append(cross(3 + i, relay_in.at[:, cols], far_in.at[:, cols]))
        if i == 0:
            wide(other, gate_send, gate_grad)
            passed.append(pass_on(0, gate_send, gate_got))
        elif i == 1:
            wide(other, up_send, up_grad)
            passed.append(pass_on(1, up_send, up_got))
        elif i == 2:
            tall(other, down_send)
            passed.append(pass_on(2, down_send, down_got))
    relay_prob[...] = prob_table(1)
    crossed.append(cross(7, relay_prob, far_prob))
    wide(side, gw, gate_grad)
    wide(side, uw, up_grad)
    tall(side, dw)
    for copy, got, sink in zip(passed, (gate_got, up_got, down_got), (gw, uw, dw)):
        copy.wait_recv()
        steps = sink.shape[0] // 128

        def add(r, carry, got=got, sink=sink):
            at = pl.ds(pl.multiple_of(r * 128, 128), 128)
            sink[at, :] = (sink[at, :].astype(F32) + got[at, :].astype(F32)).astype(BF16)
            return carry

        lax.fori_loop(0, steps, add, 0)

    arrive(back0)
    prob_out[team] = prob_table(0)
    for i in range(4):
        crossed[3 + i].wait_recv()
        combine(0, in_out, i * strip, strip, far_in)
    crossed[7].wait_recv()
    prob_out[1 - team] = far_prob[...]
    for copies, own in (in0, grad0, in1, grad1, back0, *back1):
        for copy in copies:
            copy.wait_send()
    for copy in crossed:
        copy.wait_send()
    for copy, own in exchanged:
        copy.wait_send()
    for copy in passed:
        copy.wait_send()


def fused(hidden_in, out_grad, routes, probs, w_gate, w_up, w_down):
    tok, top = routes.shape
    width = hidden_in.shape[1]
    ep = lax.axis_size("ep")
    ff = w_gate.shape[2]
    cap = 2 * tok * top // ep
    quad = ep // 2
    rows = ep * cap
    picks, place, weight = routing(routes, probs, ep)
    table = jnp.concatenate(
        [place.T.astype(F32).reshape(2, quad, tok), weight.T.reshape(2, quad, tok)], axis=1
    )
    vmem = pl.BlockSpec(memory_space=pltpu.VMEM)
    hbm = pl.BlockSpec(memory_space=pl.ANY)

    def buf(*shape, dtype=BF16):
        return pltpu.VMEM(shape, dtype)

    wide, down = (width // 2, ff), (ff // 2, width)
    dma = pltpu.SemaphoreType.DMA
    input_grad, back_prob, gw, uw, dw = pl.pallas_call(
        functools.partial(kernel, quad, cap),
        out_shape=(
            jax.ShapeDtypeStruct((tok, width), BF16),
            jax.ShapeDtypeStruct((2, ep, tok), F32),
            jax.ShapeDtypeStruct(wide, BF16),
            jax.ShapeDtypeStruct(wide, BF16),
            jax.ShapeDtypeStruct(down, BF16),
        ),
        in_specs=[vmem] * 3 + [hbm] * 3,
        out_specs=(vmem,) * 5,
        scratch_shapes=[
            buf(rows, width), buf(rows, width + LANE), buf(rows, width), buf(rows, width + LANE),
            buf(rows, width + LANE), buf(rows, width + LANE),
            buf(width, ff), buf(width, ff), buf(ff, width),
            buf(rows, ff, dtype=F32), buf(rows, ff, dtype=F32), buf(rows, ff, dtype=F32),
            buf(rows, ff), buf(rows, ff), buf(rows, ff),
            buf(*wide), buf(*wide), buf(*down), buf(*wide), buf(*wide), buf(*down),
            buf(ep, tok, dtype=F32), buf(tok, width), buf(tok, width), buf(rows, tok),
            buf(tok, width), buf(tok, width), buf(ep, tok, dtype=F32), buf(ep, tok, dtype=F32),
            dma((6, 2, quad)), dma((6, 2, quad)), dma((6, 2)),
            dma((3,)), dma((3,)), dma((3,)), dma((3,)), dma((3,)), dma((8,)), dma((8,)),
        ],
        compiler_params=pltpu.CompilerParams(
            collective_id=0, has_side_effects=True, vmem_limit_bytes=60 << 20
        ),
        cost_estimate=pl.CostEstimate(
            flops=16 * rows * width * ff, bytes_accessed=24 * rows * width, transcendentals=rows * ff
        ),
    )(hidden_in, out_grad, table, w_gate[0], w_up[0], w_down[0])
    by_expert = back_prob[:, :quad].reshape(ep, tok).T
    prob_grad = jnp.sum(jnp.where(picks, by_expert[:, None, :], 0.0), axis=2)
    return input_grad, prob_grad, gw[None], uw[None], dw[None]


def local(*arrays):
    tok, top = arrays[2].shape
    width, ff = arrays[4].shape[1] * 2, arrays[4].shape[2]
    ep = lax.axis_size("ep")
    whole_tiles = tok % 128 == 0 and width % 2048 == 0 and ff % 256 == 0
    one_each = arrays[4].shape[0] == 1 and lax.axis_size("edp") == 2
    if one_each and whole_tiles and ep == 8 and tok == LANE and 2 * tok * top // ep % 32 == 0:
        return fused(*arrays)
    return general(*arrays)


def solution(mesh):
    tokens = P(("groups", "ep", "edp"), None)
    weights = P("ep", "edp", None)
    grads = P(("groups", "ep"), "edp", None)
    return jax.shard_map(
        local,
        mesh=mesh,
        in_specs=(tokens,) * 4 + (weights,) * 3,
        out_specs=(tokens, tokens, grads, grads, grads),
        check_vma=False,
    )
```
